256 devices in a mesh: dp: 64 (over x, y, z_hi), tensor: 4 (over z_lo, core).
Axes of the slice: x: 4, y: 4, z: 8 (z_hi: 4, z_lo: 2; z = z_hi * 2 + z_lo), core: 2. Of those that a mesh axis runs over, the one named last changes fastest.
Arguments:
- mlp_input: bfloat16 [64, 512, 4608], P('dp'), may hold values from -64 to 64
- mlp_cotangent: bfloat16 [64, 512, 36864], P('dp', None, 'tensor'), may hold values from -64 to 64
- head_outputs: bfloat16 [64, 512, 2048], P('dp', None, 'tensor'), may hold values from -64 to 64
- out_cotangent: bfloat16 [64, 512, 4608], P('dp'), may hold values from -64 to 64
Outputs:
- proj_gradient: float32 [4608, 2048], P('dp', 'tensor')
- clip_factors: float32 [64], P('dp')
The draws below stay inside these ranges and needn't reach their ends.
All inputs are finite; a program needn't handle non-finite values.
Results may differ from the reference program's by a relative error of at most 0.0003.
Values may be sent and summed in bfloat16 or wider, within the bound.
A program may use at most 192 MiB of HBM per device.

```python
import math
import jax
import jax.numpy as jnp
from jax import lax

D = 4608
FF = 36864
SEQ = 512
HD = 2048
EXAMPLES = 64


def shaped_field(key, noise, width, rise, common):
    keys = jax.random.split(key, 4)
    example_scale = jnp.exp(jax.random.uniform(keys[0], (EXAMPLES, 1, 1), jnp.float32, math.log(0.25), math.log(4.0)))
    token_scale = jnp.exp(jax.random.uniform(keys[1], (EXAMPLES, SEQ, 1), jnp.float32, math.log(0.4), math.log(4.0)))
    column_scale = jnp.exp(jax.random.uniform(keys[2], (1, 1, width), jnp.float32, math.log(0.4), math.log(4.0)))
    position = jnp.arange(width, dtype=jnp.float32) / max(width - 1, 1)
    column_scale = column_scale * jnp.exp(math.log(rise) * position)[None, None, :]
    shared = jax.random.normal(keys[3], (EXAMPLES, 1, width), jnp.float32)
    value = example_scale * token_scale * column_scale * (common * shared + noise)
    return jnp.clip(value, -64.0, 64.0)


def draw_mlp_input(key, part):
    key = jax.random.fold_in(key, 11)
    first, second = jax.random.split(key)
    noise = jax.random.normal(second, (EXAMPLES, SEQ, D), jnp.float32)
    return shaped_field(first, noise, D, 1.0, 0.5).astype(jnp.bfloat16)


def draw_mlp_cotangent(key, part):
    key = jax.random.fold_in(key, 23)
    first, second = jax.random.split(key)
    noise = jax.random.normal(second, (EXAMPLES, SEQ, FF), jnp.float32)
    return shaped_field(first, noise, FF, 3.0, 0.5).astype(jnp.bfloat16)


def draw_head_outputs(key, part):
    key = jax.random.fold_in(key, 37)
    first, second = jax.random.split(key)
    noise = jax.random.normal(second, (EXAMPLES, SEQ, HD), jnp.float32)
    return shaped_field(first, noise, HD, 3.0, 0.5).astype(jnp.bfloat16)


def draw_out_cotangent(key, part):
    key = jax.random.fold_in(key, 41)
    first, second, third = jax.random.split(key, 3)
    pairing = jax.random.permutation(third, EXAMPLES)
    block = jnp.arange(D) * EXAMPLES // D
    boost = 1.0 + 2.0 * (block[None, :] == pairing[:, None]).astype(jnp.float32)
    noise = jax.random.normal(second, (EXAMPLES, SEQ, D), jnp.float32)
    value = shaped_field(first, noise, D, 1.0, 0.5)
    return jnp.clip(2.0 * value * boost[:, None, :], -64.0, 64.0).astype(jnp.bfloat16)


def setup_inputs(seed: int = 0) -> dict:
    splits = jax.random.split(jax.random.key(seed), 5)
    mlp_input = draw_mlp_input(jax.random.fold_in(splits[4], 71), 0)
    mlp_cotangent = draw_mlp_cotangent(jax.random.fold_in(splits[4], 71), 0)
    head_outputs = draw_head_outputs(jax.random.fold_in(splits[4], 71), 0)
    out_cotangent = draw_out_cotangent(jax.random.fold_in(splits[4], 71), 0)
    return dict(mlp_input=mlp_input, mlp_cotangent=mlp_cotangent, head_outputs=head_outputs, out_cotangent=out_cotangent)


def token_gram(values):
    return jnp.dot(values, values.T, preferred_element_type=jnp.float32)

def reference(mlp_input, mlp_cotangent, head_outputs, out_cotangent):
    threshold = 0.5 * SEQ * math.sqrt(D * FF + 4 * HD * D)
    factor = math.sqrt(D * HD / EXAMPLES) / threshold

    def example_norm(pieces):
        inputs_one, grads_one, heads_one, outs_one = pieces
        first = jnp.sum(token_gram(inputs_one) * token_gram(grads_one))
        second = jnp.sum(token_gram(heads_one) * token_gram(outs_one))
        return first + second
    squared = lax.map(example_norm, (mlp_input, mlp_cotangent, head_outputs, out_cotangent))
    clip_factors = threshold / jnp.maximum(jnp.sqrt(squared), threshold)
    weights = clip_factors * factor

    def add_example(running, pieces):
        outs_one, heads_one, weight_one = pieces
        product = jnp.dot(outs_one.T, heads_one, preferred_element_type=jnp.float32)
        return (running + weight_one * product, None)
    gradient, unused = lax.scan(add_example, jnp.zeros((D, HD), jnp.float32), (out_cotangent, head_outputs, weights))
    return (gradient, clip_factors)
```

```python
import functools
import math

import jax
import jax.numpy as jnp
from jax import lax
from jax.experimental import pallas as pl
from jax.experimental.pallas import tpu as pltpu
from jax.sharding import PartitionSpec as P

D = 4608
FF = 36864
HD = 2048
SEQ = 512
EXAMPLES = 64
OWNED = D // EXAMPLES
COLS = 512
HALF = SEQ // 2
MESH = pl.DeviceIdType.MESH

X0, X1, Y0, Y1, Z0, Z1 = (0, 0), (0, 1), (1, 0), (1, 1), (2, 0), (2, 1)
TURNS = (X0, X1, Y0, Y1, Z0, Z1)
PARTS = (
    ((X0, Y0, X1, Y1, Z0, Z1), 0, 56, 0, 128),
    ((Y0, X1, Y1, X0, Z1, Z0), 0, 56, 128, 128),
    ((X1, Y1, X0, Y0, Z0, Z1), 0, 56, 256, 128),
    ((Y1, X0, Y0, X1, Z1, Z0), 0, 56, 384, 128),
    ((Z0, Z1, X0, Y0, X1, Y1), 56, 16, 0, 256),
    ((Z1, Z0, Y1, X1, Y0, X0), 56, 16, 256, 256),
)
STAGES = 6
POWER = 12
TOP = 1400.0
UP = 1.004
TINY = 1e-30


def left(stage):
    return EXAMPLES >> stage


def offset(rows, stage):
    return sum(left(s) * rows + 16 for s in range(1, stage))


def turn(v, kind, bit):
    step = 1 - 2 * lax.rem(v, 2) if kind == 0 else 3 - 2 * v
    return v + bit * step


def tiles(block):
    return block.reshape(block.shape[0] // 8, 8, block.shape[1])


def flat(block):
    return block.reshape(block.shape[0] * 8, block.shape[2])


def encode(block, inverse):
    v = tiles(block) * inverse[None]
    v2 = v * v
    v4 = v2 * v2
    power = v4 * v4 * v4
    return flat(jnp.where(v < 0, -power, power)).astype(jnp.bfloat16)


def decode(raw, scale):
    power = raw.astype(jnp.float32)
    v = jnp.exp2(jnp.log2(jnp.abs(power)) * (1.0 / POWER))
    return flat(tiles(jnp.where(power < 0, -v, v)) * scale[None])


def kernel(
    threshold,
    factor,
    mlp_in,
    mlp_cot,
    heads_in,
    out_cot,
    grad,
    clip,
    x_buf,
    c_buf,
    h_buf,
    o_buf,
    prod,
    gram_x,
    gram_c,
    squares,
    largest,
    bounds_a,
    bounds_b,
    send_a,
    recv_a,
    send_b,
    recv_b,
    last_send_a,
    last_recv_a,
    last_send_b,
    last_recv_b,
    norms,
    weight_out,
    weights,
    in_sem,
    o_sem,
    x_sem,
    c_sem,
    send_sem,
    recv_sem,
    norm_send_sem,
    norm_recv_sem,
    weight_send_sem,
    weight_recv_sem,
):
    me_dp = lax.axis_index("dp")
    me_t = lax.axis_index("tensor")
    place = (lax.div(me_dp, 16), lax.rem(lax.div(me_dp, 4), 4), lax.rem(me_dp, 4))

    def index_of(at):
        return at[0] * 16 + at[1] * 4 + at[2]

    def partner(which):
        at = list(place)
        axis, kind = which
        at[axis] = turn(at[axis], kind, 1)
        return (index_of(at), me_t)

    o_step, x_step, c_step = 512, D // 2, 2304
    o_copies = [
        pltpu.make_async_copy(
            out_cot.at[0, :, pl.ds(i * o_step, o_step)],
            o_buf.at[:, pl.ds(i * o_step, o_step)],
            o_sem.at[i],
        )
        for i in range(D // o_step)
    ]
    x_copies = [
        pltpu.make_async_copy(
            mlp_in.at[0, :, pl.ds(i * x_step, x_step)],
            x_buf.at[:, pl.ds(i * x_step, x_step)],
            x_sem.at[i],
        )
        for i in range(2)
    ]
    c_copies = [
        pltpu.make_async_copy(
            mlp_cot.at[0, :, pl.ds(i * c_step, c_step)],
            c_buf.at[:, pl.ds(i * c_step, c_step)],
            c_sem.at[i],
        )
        for i in range(4)
    ]
    h_copy = pltpu.make_async_copy(heads_in.at[0], h_buf, in_sem.at[0])
    h_copy.start()
    for copy in o_copies + x_copies + c_copies:
        copy.start()

    barrier = pltpu.get_barrier_semaphore()
    peers = [partner(w) for w in TURNS]
    mates = [(me_dp, lax.rem(me_t + i, 4)) for i in range(1, 4)]
    for device in peers + mates:
        pl.semaphore_signal(barrier, inc=1, device_id=device, device_id_type=MESH)

    squares[...] = jnp.zeros_like(squares)
    largest[...] = jnp.zeros_like(largest)
    h_copy.wait()

    def product(i, carry):
        at = pl.multiple_of(i * o_step, o_step)
        pltpu.make_async_copy(
            out_cot.at[0, :, pl.ds(at, o_step)],
            o_buf.at[:, pl.ds(at, o_step)],
            o_sem.at[i],
        ).wait()
        block = lax.dot_general(
            o_buf[:, pl.ds(at, o_step)],
            h_buf[...],
            (((0,), (0,)), ((), ())),
            preferred_element_type=jnp.float32,
        )
        prod[pl.ds(at, o_step), :] = block
        block = tiles(block)
        squares[...] += jnp.sum(block * block, axis=0)
        largest[...] = jnp.maximum(largest[...], jnp.max(jnp.abs(block), axis=0))
        return carry

    lax.fori_loop(0, D // o_step, product, 0)
    pl.semaphore_wait(barrier, len(TURNS) + 3)

    def buffers(p, stage, sending):
        rows, columns = PARTS[p][2], PARTS[p][4]
        if stage == STAGES:
            if p < 4:
                return (last_send_a if sending else last_recv_a).at[p]
            return (last_send_b if sending else last_recv_b).at[p - 4]
        whole = (send_a if sending else recv_a).at[p] if p < 4 else (send_b if sending else recv_b).at[p - 4]
        return whole.at[pl.ds(offset(rows, stage), left(stage) * rows + 16)]

    def message(p, stage):
        return pltpu.make_async_remote_copy(
            src_ref=buffers(p, stage, True),
            dst_ref=buffers(p, stage, False),
            send_sem=send_sem.at[p, stage - 1],
            recv_sem=recv_sem.at[p, stage - 1],
            device_id=peers[TURNS.index(PARTS[p][0][stage - 1])],
            device_id_type=MESH,
        )

    def bound(p):
        return bounds_a.at[p] if p < 4 else bounds_b.at[p - 4]

    def rows_of(p, stage, group, k):
        order = PARTS[p][0][stage:]
        count = len(order)
        at = list(place)
        for i, (axis, kind) in enumerate(order):
            weight = 1 << (count - 1 - i)
            if weight >= 4:
                bit = lax.rem(lax.div(group, weight // 4), 2)
                at[axis] = turn(at[axis], kind, bit)
            elif (k // weight) % 2:
                at[axis] = turn(at[axis], kind, 1)
        start = index_of(at) * OWNED + PARTS[p][1]
        return pl.ds(pl.multiple_of(start, 8), PARTS[p][2])

    def columns_of(p):
        return pl.ds(PARTS[p][3], PARTS[p][4])

    def own(p, stage, group, ks):
        return jnp.concatenate(
            [prod[rows_of(p, stage, group, k), columns_of(p)] for k in ks], axis=0
        )

    def scale_out(p, stage):
        sent = (bound(p)[...] * UP).astype(jnp.bfloat16)
        rows = PARTS[p][2]
        buffers(p, stage, True)[pl.ds(left(stage) * rows, 16), :] = jnp.concatenate([sent, sent], axis=0)
        return 1.0 / sent.astype(jnp.float32)

    for p in range(len(PARTS)):
        rows = PARTS[p][2]
        bound(p)[...] = jnp.maximum(largest[:, columns_of(p)] * (1.0 / TOP), TINY)
        inverse = scale_out(p, 1)
        target = buffers(p, 1, True)

        def first(g, carry, p=p, rows=rows, inverse=inverse, target=target):
            block = own(p, 0, g + 8, range(4))
            target[pl.ds(pl.multiple_of(g * 4 * rows, 16), 4 * rows), :] = encode(block, inverse)
            return carry

        lax.fori_loop(0, 8, first, 0)
        message(p, 1).start()

    def grams(copies, buf, out, step):
        for i, copy in enumerate(copies):
            copy.wait()
            low = buf[pl.ds(0, HALF), pl.ds(i * step, step)]
            high = buf[pl.ds(HALF, HALF), pl.ds(i * step, step)]
            for j, (a, b) in enumerate(((low, low), (high, high), (low, high))):
                block = lax.dot_general(
                    a, b, (((1,), (1,)), ((), ())), preferred_element_type=jnp.float32
                )
                out[j] = block if i == 0 else out[j] + block

    grams(x_copies, x_buf, gram_x, x_step)
    grams(c_copies, c_buf, gram_c, c_step)
    both = gram_x[0] * gram_c[0] + gram_x[1] * gram_c[1] + 2.0 * (gram_x[2] * gram_c[2])
    both = jnp.sum(tiles(both), axis=0)
    attn = squares[...]
    partial = both[:, :128] + both[:, 128:]
    for i in range(4):
        partial = partial + attn[:, 128 * i : 128 * (i + 1)]
    norms[me_t] = partial
    shares = [
        pltpu.make_async_remote_copy(
            src_ref=norms.at[me_t],
            dst_ref=norms.at[me_t],
            send_sem=norm_send_sem.at[i],
            recv_sem=norm_recv_sem.at[i],
            device_id=mates[i],
            device_id_type=MESH,
        )
        for i in range(3)
    ]
    for copy in shares:
        copy.start()
    for copy in shares:
        copy.wait()
    total = (norms[0] + norms[1]) + (norms[2] + norms[3])
    total = jnp.sum(jnp.sum(total, axis=1, keepdims=True), axis=0, keepdims=True)
    squared = jnp.broadcast_to(total, (8, 128))
    factors = threshold / jnp.maximum(jnp.sqrt(squared), threshold)
    weight = factors * factor
    weight_out[...] = weight
    gifts = [
        pltpu.make_async_remote_copy(
            src_ref=weight_out,
            dst_ref=weights.at[i],
            send_sem=weight_send_sem.at[i],
            recv_sem=weight_recv_sem.at[i],
            device_id=peers[i],
            device_id_type=MESH,
        )
        for i in range(len(TURNS))
    ]
    for copy in gifts:
        copy.start()
    clip[0] = factors[0, 0]
    for copy in gifts:
        copy.wait()

    def wide(tile, columns):
        return tile if columns == 128 else jnp.concatenate([tile] * (columns // 128), axis=1)

    for stage in range(1, STAGES):
        kept = []
        for p in range(len(PARTS)):
            order, _, rows, _, columns = PARTS[p]
            came = buffers(p, stage, False)
            message(p, stage).wait()
            scale = came[pl.ds(left(stage) * rows, 16), :].astype(jnp.float32)[:8]
            mine = None
            if stage == 1:
                mine = wide(weight, columns)
                scale = scale * wide(weights[TURNS.index(order[0])], columns)
                bound(p)[...] = bound(p)[...] * mine + scale
            else:
                bound(p)[...] = bound(p)[...] + scale

            def summed(g, ks, p=p, stage=stage, rows=rows, came=came, scale=scale, mine=mine):
                ks = list(ks)
                block = own(p, stage, g, ks)
                if mine is not None:
                    block = flat(tiles(block) * mine[None])
                if stage == 5:
                    raw = came[pl.ds(0, 2 * rows), :]
                    theirs = decode(raw, scale)[ks[0] * rows : (ks[-1] + 1) * rows]
                else:
                    start = g * 4 * rows + ks[0] * rows
                    theirs = decode(came[pl.ds(pl.multiple_of(start, 16), len(ks) * rows), :], scale)
                return block + theirs

            target = buffers(p, stage + 1, True)
            groups = left(stage) // 8
            if stage < 4:
                inverse = scale_out(p, stage + 1)

                def send(g, carry, rows=rows, groups=groups, target=target, inverse=inverse, summed=summed):
                    block = summed(g + groups, range(4))
                    target[pl.ds(pl.multiple_of(g * 4 * rows, 16), 4 * rows), :] = encode(block, inverse)
                    return carry

                lax.fori_loop(0, groups, send, 0)
            elif stage == 4:
                inverse = scale_out(p, stage + 1)
                target[pl.ds(0, 2 * rows), :] = encode(summed(0, (2, 3)), inverse)
            else:
                target[...] = summed(0, (1,))
            message(p, stage + 1).start()
            kept.append((p, groups, summed))
        for p, groups, summed in kept:
            rows = PARTS[p][2]

            def keep(g, carry, p=p, stage=stage, rows=rows, summed=summed, ks=(0, 1, 2, 3)):
                block = summed(g, ks)
                for i, k in enumerate(ks):
                    prod[rows_of(p, stage, g, k), columns_of(p)] = block[i * rows : (i + 1) * rows]
                return carry

            if stage < 4:
                lax.fori_loop(0, groups, keep, 0)
            else:
                keep(0, 0, ks=(0, 1) if stage == 4 else (0,))

    for p in range(len(PARTS)):
        message(p, STAGES).wait()
        rows = PARTS[p][2]
        block = prod[rows_of(p, STAGES, 0, 0), columns_of(p)] + buffers(p, STAGES, False)[...]
        grad[pl.ds(PARTS[p][1], rows), columns_of(p)] = block


def on_device(mlp_input, mlp_cotangent, head_outputs, out_cotangent):
    threshold = 0.5 * SEQ * math.sqrt(D * FF + 4 * HD * D)
    factor = math.sqrt(D * HD / EXAMPLES) / threshold
    rows_a = offset(56, STAGES)
    rows_b = offset(16, STAGES)
    f32, bf16 = jnp.float32, jnp.bfloat16
    dma = pltpu.SemaphoreType.DMA
    return pl.pallas_call(
        functools.partial(kernel, threshold, factor),
        out_shape=(
            jax.ShapeDtypeStruct((OWNED, COLS), f32),
            jax.ShapeDtypeStruct((1,), f32),
        ),
        in_specs=[pl.BlockSpec(memory_space=pl.ANY)] * 4,
        out_specs=(
            pl.BlockSpec(memory_space=pltpu.VMEM),
            pl.BlockSpec(memory_space=pltpu.SMEM),
        ),
        scratch_shapes=[
            pltpu.VMEM((SEQ, D), bf16),
            pltpu.VMEM((SEQ, FF // 4), bf16),
            pltpu.VMEM((SEQ, COLS), bf16),
            pltpu.VMEM((SEQ, D), bf16),
            pltpu.VMEM((D, COLS), f32),
            pltpu.VMEM((3, HALF, HALF), f32),
            pltpu.VMEM((3, HALF, HALF), f32),
            pltpu.VMEM((8, COLS), f32),
            pltpu.VMEM((8, COLS), f32),
            pltpu.VMEM((4, 8, 128), f32),
            pltpu.VMEM((2, 8, 256), f32),
            pltpu.VMEM((4, rows_a, 128), bf16),
            pltpu.VMEM((4, rows_a, 128), bf16),
            pltpu.VMEM((2, rows_b, 256), bf16),
            pltpu.VMEM((2, rows_b, 256), bf16),
            pltpu.VMEM((4, 56, 128), f32),
            pltpu.VMEM((4, 56, 128), f32),
            pltpu.VMEM((2, 16, 256), f32),
            pltpu.VMEM((2, 16, 256), f32),
            pltpu.VMEM((4, 8, 128), f32),
            pltpu.VMEM((8, 128), f32),
            pltpu.VMEM((6, 8, 128), f32),
            dma((1,)),
            dma((D // 512,)),
            dma((2,)),
            dma((4,)),
            dma((6, 6)),
            dma((6, 6)),
            dma((3,)),
            dma((3,)),
            dma((6,)),
            dma((6,)),
        ],
        compiler_params=pltpu.CompilerParams(
            collective_id=0,
            has_side_effects=True,
            vmem_limit_bytes=56 * 2**20,
        ),
    )(mlp_input, mlp_cotangent, head_outputs, out_cotangent)


def solution(mesh):
    return jax.shard_map(
        on_device,
        mesh=mesh,
        in_specs=(
            P("dp", None, None),
            P("dp", None, "tensor"),
            P("dp", None, "tensor"),
            P("dp", None, None),
        ),
        out_specs=(P("dp", "tensor"), P("dp")),
        check_vma=False,
    )
```

```python
import functools
import itertools
import math

import jax
import jax.numpy as jnp
from jax import lax
from jax.experimental import pallas as pl
from jax.experimental.pallas import tpu as pltpu
from jax.sharding import PartitionSpec as P

D = 4608
FF = 36864
HD = 2048
SEQ = 512
EXAMPLES = 64
OWNED = D // EXAMPLES
COLS = 512
LANES = 128
HALF = SEQ // 2
MESH = pl.DeviceIdType.MESH

X0, X1, Y0, Y1, Z0, Z1 = (0, 0), (0, 1), (1, 0), (1, 1), (2, 0), (2, 1)
TURNS = (X0, X1, Y0, Y1, Z0, Z1)
ALONG_Z = (Z0, Z1)
PLANE = (X0, X1, Y0, Y1)
ORDERS = (
    ((X0,), (Y0,), (X1, Y1), ALONG_Z),
    ((Y0,), (X1,), (Y1, X0), ALONG_Z),
    ((X1,), (Y1,), (X0, Y0), ALONG_Z),
    ((Y1,), (X0,), (Y0, X1), ALONG_Z),
    ((Z0,), (Z1,), PLANE),
    ((Z1,), (Z0,), PLANE),
)
PARTS = (
    (0, 0, 32, 0),
    (1, 32, 24, 0),
    (2, 0, 32, 1),
    (3, 32, 24, 1),
    (4, 56, 16, 0),
    (5, 56, 16, 1),
    (1, 0, 32, 2),
    (0, 32, 24, 2),
    (3, 0, 32, 3),
    (2, 32, 24, 3),
    (4, 56, 16, 2),
    (5, 56, 16, 3),
)
XY = ((0, 1, 2, 3), (6, 7, 8, 9))
Z = ((4, 5), (10, 11))
Z_ALL = Z[0] + Z[1]
SCALE_ROWS = 16
POWER = 12
TOP = 1400.0
UP = 1.004
TINY = 1e-30


def layout():
    table, row = {}, 0

    def add(key, rows, turns):
        nonlocal row
        table[key] = (row, rows, turns)
        row += rows + SCALE_ROWS

    def reached(turns):
        for tau in range(1, 1 << len(turns)):
            bits = [(tau >> (len(turns) - 1 - i)) & 1 for i in range(len(turns))]
            yield tau, tuple(t for t, b in zip(turns, bits) if b)

    for p, (order, _, rows, _) in enumerate(PARTS):
        steps = ORDERS[order]
        add((p, 0, 1), 32 * rows, steps[0])
        add((p, 1, 1), 16 * rows, steps[1])
        if len(steps) == 4:
            for tau, turns in reached(steps[2]):
                add((p, 2, tau), 4 * rows, turns)
    for half in range(2):
        for tau, turns in reached(ALONG_Z):
            add(("xy", half, tau), sum(PARTS[p][2] for p in XY[half]), turns)
    for tau, turns in reached(PLANE):
        add(("z", 0, tau), sum(PARTS[p][2] for p in Z_ALL), turns)
    return table, row


MESSAGES, MESSAGE_ROWS = layout()
NUMBER = {key: i for i, key in enumerate(MESSAGES)}


def turn(v, kind, bit):
    step = 1 - 2 * lax.rem(v, 2) if kind == 0 else 3 - 2 * v
    return v + bit * step


def tiles(block):
    return block.reshape(block.shape[0] // 8, 8, block.shape[1])


def flat(block):
    return block.reshape(block.shape[0] * 8, block.shape[2])


def encode(block, inverse):
    v = tiles(block) * inverse[None]
    v2 = v * v
    v4 = v2 * v2
    power = v4 * v4 * v4
    return flat(jnp.where(v < 0, -power, power)).astype(jnp.bfloat16)


def decode(power, scale):
    v = jnp.exp2(jnp.log2(jnp.abs(power)) * (1.0 / POWER))
    return flat(tiles(jnp.where(power < 0, -v, v)) * scale[None])


def kernel(
    threshold,
    factor,
    mlp_in,
    mlp_cot,
    heads_in,
    out_cot,
    grad,
    clip,
    x_buf,
    c_buf,
    h_buf,
    o_buf,
    prod,
    gram_x,
    gram_c,
    squares,
    largest,
    bounds,
    outgoing,
    incoming,
    norm_out,
    norm_mate,
    norms,
    weights,
    in_sem,
    o_sem,
    c_sem,
    send_sem,
    recv_sem,
    mate_send,
    mate_recv,
    norm_send,
    norm_recv,
):
    me_dp = lax.axis_index("dp")
    me_t = lax.axis_index("tensor")
    core = lax.rem(me_t, 2)
    chip = lax.div(me_t, 2)
    place = (lax.div(me_dp, 16), lax.rem(lax.div(me_dp, 4), 4), lax.rem(me_dp, 4))

    def index_of(at):
        return at[0] * 16 + at[1] * 4 + at[2]

    def turned(turns):
        at = list(place)
        for axis, kind in turns:
            at[axis] = turn(at[axis], kind, 1)
        return index_of(at)

    o_step, c_step = 1536, D
    blocks = D // o_step

    def columns(source, target, start, size, sem):
        return pltpu.make_async_copy(
            source.at[0, :, pl.ds(start, size)], target.at[:, pl.ds(start, size)], sem
        )

    h_copy = pltpu.make_async_copy(heads_in.at[0], h_buf, in_sem.at[0])
    x_copy = pltpu.make_async_copy(mlp_in.at[0], x_buf, in_sem.at[1])
    o_copies = [columns(out_cot, o_buf, i * o_step, o_step, o_sem.at[i]) for i in range(blocks)]
    c_copies = [columns(mlp_cot, c_buf, i * c_step, c_step, c_sem.at[i]) for i in range(2)]
    for copy in [h_copy, *o_copies, x_copy, *c_copies]:
        copy.start()

    barrier = pltpu.get_barrier_semaphore()
    other_chip = lax.rem(me_t + 2, 4)
    other_core = (me_dp, turn(me_t, 0, 1))
    subsets = [s for n in range(1, 5) for s in itertools.combinations(PLANE, n)]
    subsets += [(Z0,), (Z1,), ALONG_Z]
    greeted = [(turned(s), me_t) for s in subsets]
    greeted += [(turned((t,)), other_chip) for t in TURNS]
    greeted += [(me_dp, other_chip), other_core]
    for device in greeted:
        pl.semaphore_signal(barrier, inc=1, device_id=device, device_id_type=MESH)

    def rows_of_message(key, ref):
        start, rows, _ = MESSAGES[key]
        return ref.at[pl.ds(start, rows + SCALE_ROWS)]

    def message(key):
        n = NUMBER[key]
        return pltpu.make_async_remote_copy(
            src_ref=rows_of_message(key, outgoing),
            dst_ref=rows_of_message(key, incoming),
            send_sem=send_sem.at[n],
            recv_sem=recv_sem.at[n],
            device_id=(turned(MESSAGES[key][2]), me_t),
            device_id_type=MESH,
        )

    def put_scale(key, sent):
        start, rows, _ = MESSAGES[key]
        outgoing[pl.ds(start + rows, SCALE_ROWS), :] = jnp.concatenate([sent, sent], axis=0)

    def put(key, at, block, inverse):
        start = MESSAGES[key][0]
        outgoing[pl.ds(pl.multiple_of(start + at, 16), block.shape[0]), :] = encode(block, inverse)

    def scale_in(key):
        start, rows, _ = MESSAGES[key]
        return incoming[pl.ds(start + rows, SCALE_ROWS), :].astype(jnp.float32)[:8]

    def got(key, at, size, scale):
        start = pl.multiple_of(MESSAGES[key][0] + at, 16)
        return decode(incoming[pl.ds(start, size), :].astype(jnp.float32), scale)

    def got_within(key, at, size, scale):
        low, high = at // 16 * 16, -(-(at + size) // 16) * 16
        raw = incoming[pl.ds(MESSAGES[key][0] + low, high - low), :].astype(jnp.float32)
        return decode(raw[at - low : at - low + size], scale)

    def to_send(bound):
        sent = (bound * UP).astype(jnp.bfloat16)
        return sent, 1.0 / sent.astype(jnp.float32)

    def lanes_of(p):
        return pl.ds(PARTS[p][3] * LANES, LANES)

    def place_of(p, done, group, k):
        order = list(itertools.chain(*ORDERS[PARTS[p][0]][done:]))
        at = list(place)
        for i, (axis, kind) in enumerate(order):
            weight = 1 << (len(order) - 1 - i)
            if weight >= 4:
                at[axis] = turn(at[axis], kind, lax.rem(lax.div(group, weight // 4), 2))
            elif (k // weight) % 2:
                at[axis] = turn(at[axis], kind, 1)
        start = index_of(at) * OWNED + PARTS[p][1]
        return pl.ds(pl.multiple_of(start, 8), PARTS[p][2])

    def own(p, done, group, ks):
        return jnp.concatenate([prod[place_of(p, done, group, k), lanes_of(p)] for k in ks], axis=0)

    def keep(p, done, group, ks, block):
        rows = PARTS[p][2]
        for i, k in enumerate(ks):
            prod[place_of(p, done, group, k), lanes_of(p)] = block[i * rows : (i + 1) * rows]

    ALL4 = range(4)
    h_copy.wait()
    for half in range(2):
        part = pl.ds(half * 256, 256)
        for i in range(blocks):
            if half == 0:
                o_copies[i].wait()
            block = lax.dot_general(
                o_buf[:, pl.ds(i * o_step, o_step)],
                h_buf[:, part],
                (((0,), (0,)), ((), ())),
                preferred_element_type=jnp.float32,
            )
            prod[pl.ds(i * o_step, o_step), part] = block
            block = tiles(block)
            square = jnp.sum(block * block, axis=0)
            most = jnp.max(jnp.abs(block), axis=0)
            squares[:, part] = square if i == 0 else squares[:, part] + square
            largest[:, part] = most if i == 0 else jnp.maximum(largest[:, part], most)
        if half == 0:
            pl.semaphore_wait(barrier, len(greeted))
        for p in Z[half] + XY[half]:
            rows = PARTS[p][2]
            bound = jnp.maximum(largest[:, lanes_of(p)] * (1.0 / TOP), TINY)
            bounds[p] = bound
            sent, inverse = to_send(bound)
            put_scale((p, 0, 1), sent)

            def first(g, carry, p=p, rows=rows, inverse=inverse):
                put((p, 0, 1), g * 4 * rows, own(p, 0, g + 8, ALL4), inverse)
                return carry

            lax.fori_loop(0, 8, first, 0)
            message((p, 0, 1)).start()

    nt = (((1,), (1,)), ((), ()))

    def gram(a, b):
        return lax.dot_general(a, b, nt, preferred_element_type=jnp.float32)

    x_copy.wait()
    mine = x_buf[pl.ds(pl.multiple_of(core * HALF, HALF), HALF), :]
    gram_x[core] = gram(mine, mine)
    quarter = pl.ds(pl.multiple_of(core * 128, 128), 128)
    gram_x[2, quarter, :] = gram(x_buf[quarter, :], x_buf[pl.ds(HALF, HALF), :])

    def to_core(source, target, n):
        return pltpu.make_async_remote_copy(
            src_ref=source,
            dst_ref=target,
            send_sem=mate_send.at[n],
            recv_sem=mate_recv.at[n],
            device_id=other_core,
            device_id_type=MESH,
        )

    grams_out = [
        to_core(gram_x.at[core], gram_x.at[core], 0),
        to_core(gram_x.at[2, quarter], gram_x.at[2, quarter], 1),
    ]
    for copy in grams_out:
        copy.start()
    attn = squares[...]
    partial = (attn[:, :128] + attn[:, 128:256]) + (attn[:, 256:384] + attn[:, 384:])
    for i in range(2):
        c_copies[i].wait()
        low = c_buf[pl.ds(0, HALF), pl.ds(i * c_step, c_step)]
        high = c_buf[pl.ds(HALF, HALF), pl.ds(i * c_step, c_step)]
        for j, (a, b) in enumerate(((low, low), (high, high), (low, high))):
            block = gram(a, b)
            gram_c[j] = block if i == 0 else gram_c[j] + block
    for copy in grams_out:
        copy.wait()
    both = gram_x[0] * gram_c[0] + gram_x[1] * gram_c[1] + 2.0 * (gram_x[2] * gram_c[2])
    both = jnp.sum(tiles(both), axis=0)
    norm_out[0] = partial + (both[:, :128] + both[:, 128:])
    mate = to_core(norm_out.at[0], norm_mate, 2)
    mate.start()
    mate.wait_recv()
    norm_out[1] = norm_out[0] + norm_mate[...]
    norms[0, chip] = norm_out[1]
    norm_copies = []
    for device, slot in [((me_dp, other_chip), 0)] + [
        ((turned((t,)), to), i + 1) for i, t in enumerate(TURNS) for to in (me_t, other_chip)
    ]:
        n = len(norm_copies)
        norm_copies.append(
            pltpu.make_async_remote_copy(
                src_ref=norm_out.at[1],
                dst_ref=norms.at[slot, chip],
                send_sem=norm_send.at[n],
                recv_sem=norm_recv.at[n],
                device_id=device,
                device_id_type=MESH,
            )
        )
    for copy in norm_copies:
        copy.start()
    for copy in norm_copies:
        copy.wait_recv()
    total = norms[:, 0] + norms[:, 1]
    total = jnp.sum(jnp.sum(total, axis=2, keepdims=True), axis=1, keepdims=True)
    factors = threshold / jnp.maximum(jnp.sqrt(jnp.broadcast_to(total, (7, 8, 128))), threshold)
    weights[...] = factors * factor

    def second(parts):
        kept = []
        for p in parts:
            order, _, rows, _ = PARTS[p]
            came = (p, 0, 1)
            message(came).wait_recv()
            mine = weights[0]
            scale = scale_in(came) * weights[1 + TURNS.index(ORDERS[order][0][0])]
            bound = bounds[p] * mine + scale
            bounds[p] = bound
            sent, inverse = to_send(bound)
            put_scale((p, 1, 1), sent)

            def summed(g, p=p, rows=rows, came=came, mine=mine, scale=scale):
                block = flat(tiles(own(p, 1, g, ALL4)) * mine[None])
                return block + got(came, g * 4 * rows, 4 * rows, scale)

            def send(g, carry, p=p, rows=rows, inverse=inverse, summed=summed):
                put((p, 1, 1), g * 4 * rows, summed(g + 4), inverse)
                return carry

            lax.fori_loop(0, 4, send, 0)
            message((p, 1, 1)).start()
            kept.append((p, summed))
        for p, summed in kept:

            def hold(g, carry, p=p, summed=summed):
                keep(p, 1, g, ALL4, summed(g))
                return carry

            lax.fori_loop(0, 4, hold, 0)

    def third(parts):
        kept = []
        for p in parts:
            rows = PARTS[p][2]
            came = (p, 1, 1)
            message(came).wait_recv()
            scale = scale_in(came)
            bound = bounds[p] + scale
            bounds[p] = bound
            sent, inverse = to_send(bound)

            def summed(g, p=p, rows=rows, came=came, scale=scale):
                return own(p, 2, g, ALL4) + got(came, g * 4 * rows, 4 * rows, scale)

            for tau in range(1, 4):
                put_scale((p, 2, tau), sent)
                put((p, 2, tau), 0, summed(tau), inverse)
                message((p, 2, tau)).start()
            kept.append((p, summed))
        for p, summed in kept:
            keep(p, 2, 0, ALL4, summed(0))

    def fourth(half):
        scales, bound = {}, None
        for p in XY[half]:
            here = bounds[p]
            for tau in range(1, 4):
                message((p, 2, tau)).wait_recv()
                scales[p, tau] = scale_in((p, 2, tau))
                here = here + scales[p, tau]
            bound = here if bound is None else jnp.maximum(bound, here)
        sent, inverse = to_send(bound)

        def summed(p, k):
            rows = PARTS[p][2]
            block = own(p, 3, 0, (k,))
            for tau in range(1, 4):
                block = block + got_within((p, 2, tau), k * rows, rows, scales[p, tau])
            return block

        for k in range(1, 4):
            key = ("xy", half, k)
            put_scale(key, sent)
            put(key, 0, jnp.concatenate([summed(p, k) for p in XY[half]], axis=0), inverse)
            message(key).start()
        for p in XY[half]:
            keep(p, 3, 0, (0,), summed(p, 0))

    def third_z():
        scales, bound = {}, None
        for p in Z_ALL:
            message((p, 1, 1)).wait_recv()
            scales[p] = scale_in((p, 1, 1))
            here = bounds[p] + scales[p]
            bound = here if bound is None else jnp.maximum(bound, here)
        sent, inverse = to_send(bound)

        def summed(p, g, ks):
            rows = PARTS[p][2]
            return own(p, 2, g, ks) + got((p, 1, 1), g * 4 * rows + ks[0] * rows, len(ks) * rows, scales[p])

        for owner in range(1, 16):
            key = ("z", 0, owner)
            put_scale(key, sent)
            put(
                key,
                0,
                jnp.concatenate([summed(p, owner // 4, (owner % 4,)) for p in Z_ALL], axis=0),
                inverse,
            )
            message(key).start()
        for p in Z_ALL:
            keep(p, 2, 0, (0,), summed(p, 0, (0,)))

    def finish(parts, kind, half, count):
        done = len(ORDERS[PARTS[parts[0]][0]])
        block = jnp.concatenate([own(p, done, 0, (0,)) for p in parts], axis=0)
        for tau in range(1, count):
            key = (kind, half, tau)
            message(key).wait_recv()
            block = block + got(key, 0, block.shape[0], scale_in(key))
        row = 0
        for p in parts:
            _, first_row, rows, _ = PARTS[p]
            grad[pl.ds(first_row, rows), lanes_of(p)] = block[row : row + rows]
            row += rows

    second(XY[0])
    second(XY[1])
    second(Z_ALL)
    third(XY[0])
    third(XY[1])
    fourth(0)
    third_z()
    fourth(1)
    finish(XY[0], "xy", 0, 4)
    finish(Z_ALL, "z", 0, 16)
    finish(XY[1], "xy", 1, 4)
    clip[0] = factors[0, 0, 0]
    for key in MESSAGES:
        message(key).wait_send()
    for copy in [mate, *norm_copies]:
        copy.wait_send()


def on_device(mlp_input, mlp_cotangent, head_outputs, out_cotangent):
    threshold = 0.5 * SEQ * math.sqrt(D * FF + 4 * HD * D)
    factor = math.sqrt(D * HD / EXAMPLES) / threshold
    f32, bf16 = jnp.float32, jnp.bfloat16
    dma = pltpu.SemaphoreType.DMA
    return pl.pallas_call(
        functools.partial(kernel, threshold, factor),
        out_shape=(
            jax.ShapeDtypeStruct((OWNED, COLS), f32),
            jax.ShapeDtypeStruct((1,), f32),
        ),
        in_specs=[pl.BlockSpec(memory_space=pl.ANY)] * 4,
        out_specs=(
            pl.BlockSpec(memory_space=pltpu.VMEM),
            pl.BlockSpec(memory_space=pltpu.SMEM),
        ),
        scratch_shapes=[
            pltpu.VMEM((SEQ, D), bf16),
            pltpu.VMEM((SEQ, FF // 4), bf16),
            pltpu.VMEM((SEQ, COLS), bf16),
            pltpu.VMEM((SEQ, D), bf16),
            pltpu.VMEM((D, COLS), f32),
            pltpu.VMEM((3, HALF, HALF), f32),
            pltpu.VMEM((3, HALF, HALF), f32),
            pltpu.VMEM((8, COLS), f32),
            pltpu.VMEM((8, COLS), f32),
            pltpu.VMEM((len(PARTS), 8, LANES), f32),
            pltpu.VMEM((MESSAGE_ROWS, LANES), bf16),
            pltpu.VMEM((MESSAGE_ROWS, LANES), bf16),
            pltpu.VMEM((2, 8, LANES), f32),
            pltpu.VMEM((8, LANES), f32),
            pltpu.VMEM((7, 2, 8, LANES), f32),
            pltpu.VMEM((7, 8, LANES), f32),
            dma((2,)),
            dma((3,)),
            dma((2,)),
            dma((len(MESSAGES),)),
            dma((len(MESSAGES),)),
            dma((3,)),
            dma((3,)),
            dma((13,)),
            dma((13,)),
        ],
        compiler_params=pltpu.CompilerParams(
            collective_id=0,
            has_side_effects=True,
            vmem_limit_bytes=56 * 2**20,
        ),
    )(mlp_input, mlp_cotangent, head_outputs, out_cotangent)


def solution(mesh):
    return jax.shard_map(
        on_device,
        mesh=mesh,
        in_specs=(
            P("dp", None, None),
            P("dp", None, "tensor"),
            P("dp", None, "tensor"),
            P("dp", None, None),
        ),
        out_specs=(P("dp", "tensor"), P("dp")),
        check_vma=False,
    )
```

```python
import functools
import itertools
import math

import jax
import jax.numpy as jnp
from jax import lax
from jax.experimental import pallas as pl
from jax.experimental.pallas import tpu as pltpu
from jax.sharding import PartitionSpec as P

D = 4608
FF = 36864
HD = 2048
SEQ = 512
EXAMPLES = 64
OWNED = D // EXAMPLES
COLS = 512
LANES = 128
HALF = SEQ // 2
MESH = pl.DeviceIdType.MESH

X0, X1, Y0, Y1, Z0, Z1 = (0, 0), (0, 1), (1, 0), (1, 1), (2, 0), (2, 1)
TURNS = (X0, X1, Y0, Y1, Z0, Z1)
ALONG_Z = (Z0, Z1)
PLANE = (X0, X1, Y0, Y1)
ORDERS = (
    ((X0,), (Y0,), (X1, Y1), ALONG_Z),
    ((Y0,), (X1,), (Y1, X0), ALONG_Z),
    ((X1,), (Y1,), (X0, Y0), ALONG_Z),
    ((Y1,), (X0,), (Y0, X1), ALONG_Z),
    ((Z0,), (Z1,), PLANE),
    ((Z1,), (Z0,), PLANE),
)
PARTS = (
    (0, 0, 32, 0),
    (1, 32, 24, 0),
    (2, 0, 32, 1),
    (3, 32, 24, 1),
    (4, 56, 16, 0),
    (5, 56, 16, 1),
    (1, 0, 32, 2),
    (0, 32, 24, 2),
    (3, 0, 32, 3),
    (2, 32, 24, 3),
    (4, 56, 16, 2),
    (5, 56, 16, 3),
)
XY = ((0, 1, 2, 3), (6, 7, 8, 9))
Z = ((4, 5), (10, 11))
Z_ALL = Z[0] + Z[1]
SCALE_ROWS = 16
POWER = 12
TOP = 1400.0
UP = 1.004
TINY = 1e-30


def layout():
    table, row = {}, 0

    def add(key, rows, turns):
        nonlocal row
        table[key] = (row, rows, turns)
        row += rows + SCALE_ROWS

    def reached(turns):
        for tau in range(1, 1 << len(turns)):
            bits = [(tau >> (len(turns) - 1 - i)) & 1 for i in range(len(turns))]
            yield tau, tuple(t for t, b in zip(turns, bits) if b)

    for p, (order, _, rows, _) in enumerate(PARTS):
        steps = ORDERS[order]
        add((p, 0, 1), 32 * rows, steps[0])
        add((p, 1, 1), 16 * rows, steps[1])
        if len(steps) == 4:
            for tau, turns in reached(steps[2]):
                add((p, 2, tau), 4 * rows, turns)
    for half in range(2):
        for tau, turns in reached(ALONG_Z):
            add(("xy", half, tau), sum(PARTS[p][2] for p in XY[half]), turns)
    for tau, turns in reached(PLANE):
        add(("z", 0, tau), sum(PARTS[p][2] for p in Z_ALL), turns)
    return table, row


MESSAGES, MESSAGE_ROWS = layout()
NUMBER = {key: i for i, key in enumerate(MESSAGES)}


def turn(v, kind, bit):
    step = 1 - 2 * lax.rem(v, 2) if kind == 0 else 3 - 2 * v
    return v + bit * step


def tiles(block):
    return block.reshape(block.shape[0] // 8, 8, block.shape[1])


def flat(block):
    return block.reshape(block.shape[0] * 8, block.shape[2])


def encode(block, inverse):
    v = tiles(block) * inverse[None]
    v2 = v * v
    v4 = v2 * v2
    power = v4 * v4 * v4
    return flat(jnp.where(v < 0, -power, power)).astype(jnp.bfloat16)


def decode(power, scale):
    v = jnp.exp2(jnp.log2(jnp.abs(power)) * (1.0 / POWER))
    return flat(tiles(jnp.where(power < 0, -v, v)) * scale[None])


def kernel(
    threshold,
    factor,
    mlp_in,
    mlp_cot,
    heads_in,
    out_cot,
    grad,
    clip,
    x_buf,
    c_buf,
    h_buf,
    o_buf,
    prod,
    gram_x,
    gram_c,
    squares,
    largest,
    bounds,
    outgoing,
    incoming,
    norm_out,
    norm_mate,
    norms,
    weights,
    in_sem,
    o_sem,
    c_sem,
    send_sem,
    recv_sem,
    mate_send,
    mate_recv,
    norm_send,
    norm_recv,
):
    me_dp = lax.axis_index("dp")
    me_t = lax.axis_index("tensor")
    core = lax.rem(me_t, 2)
    chip = lax.div(me_t, 2)
    place = (lax.div(me_dp, 16), lax.rem(lax.div(me_dp, 4), 4), lax.rem(me_dp, 4))

    def index_of(at):
        return at[0] * 16 + at[1] * 4 + at[2]

    def turned(turns):
        at = list(place)
        for axis, kind in turns:
            at[axis] = turn(at[axis], kind, 1)
        return index_of(at)

    o_step, c_step = 1536, D
    blocks = D // o_step

    def columns(source, target, start, size, sem):
        return pltpu.make_async_copy(
            source.at[0, :, pl.ds(start, size)], target.at[:, pl.ds(start, size)], sem
        )

    h_copy = pltpu.make_async_copy(heads_in.at[0], h_buf, in_sem.at[0])
    x_copy = pltpu.make_async_copy(mlp_in.at[0], x_buf, in_sem.at[1])
    o_copies = [columns(out_cot, o_buf, i * o_step, o_step, o_sem.at[i]) for i in range(blocks)]
    c_copies = [columns(mlp_cot, c_buf, i * c_step, c_step, c_sem.at[i]) for i in range(2)]
    for copy in [h_copy, *o_copies, x_copy, *c_copies]:
        copy.start()

    barrier = pltpu.get_barrier_semaphore()
    other_chip = lax.rem(me_t + 2, 4)
    other_core = (me_dp, turn(me_t, 0, 1))
    subsets = [s for n in range(1, 5) for s in itertools.combinations(PLANE, n)]
    subsets += [(Z0,), (Z1,), ALONG_Z]
    greeted = [(turned(s), me_t) for s in subsets]
    greeted += [(turned((t,)), other_chip) for t in TURNS]
    greeted += [(me_dp, other_chip), other_core]
    for device in greeted:
        pl.semaphore_signal(barrier, inc=1, device_id=device, device_id_type=MESH)

    def rows_of_message(key, ref):
        start, rows, _ = MESSAGES[key]
        return ref.at[pl.ds(start, rows + SCALE_ROWS)]

    def message(key):
        n = NUMBER[key]
        return pltpu.make_async_remote_copy(
            src_ref=rows_of_message(key, outgoing),
            dst_ref=rows_of_message(key, incoming),
            send_sem=send_sem.at[n],
            recv_sem=recv_sem.at[n],
            device_id=(turned(MESSAGES[key][2]), me_t),
            device_id_type=MESH,
        )

    def put_scale(key, sent):
        start, rows, _ = MESSAGES[key]
        outgoing[pl.ds(start + rows, SCALE_ROWS), :] = jnp.concatenate([sent, sent], axis=0)

    def put(key, at, block, inverse):
        outgoing[pl.ds(MESSAGES[key][0] + at, block.shape[0]), :] = encode(block, inverse)

    def scale_in(key):
        start, rows, _ = MESSAGES[key]
        return incoming[pl.ds(start + rows, SCALE_ROWS), :].astype(jnp.float32)[:8]

    def got(key, at, size, scale):
        return decode(incoming[pl.ds(MESSAGES[key][0] + at, size), :].astype(jnp.float32), scale)

    def got_within(key, at, size, scale):
        low, high = at // 16 * 16, -(-(at + size) // 16) * 16
        raw = incoming[pl.ds(MESSAGES[key][0] + low, high - low), :].astype(jnp.float32)
        return decode(raw[at - low : at - low + size], scale)

    def to_send(bound):
        sent = (bound * UP).astype(jnp.bfloat16)
        return sent, 1.0 / sent.astype(jnp.float32)

    def lanes_of(p):
        return pl.ds(PARTS[p][3] * LANES, LANES)

    bases = {}
    for axis, stride in enumerate((16 * OWNED, 4 * OWNED, OWNED)):
        for zero in range(2):
            for one in range(2):
                at = place[axis]
                if zero:
                    at = turn(at, 0, 1)
                if one:
                    at = turn(at, 1, 1)
                bases[axis, zero, one] = at * stride

    def place_of(p, done, group, k):
        order = list(itertools.chain(*ORDERS[PARTS[p][0]][done:]))
        owner = 4 * group + k
        bits = {t: (owner >> (len(order) - 1 - i)) & 1 for i, t in enumerate(order)}
        start = PARTS[p][1] + sum(bases[a, bits.get((a, 0), 0), bits.get((a, 1), 0)] for a in range(3))
        return pl.ds(pl.multiple_of(start, 8), PARTS[p][2])

    def own(p, done, group, ks):
        return jnp.concatenate([prod[place_of(p, done, group, k), lanes_of(p)] for k in ks], axis=0)

    def keep(p, done, group, ks, block):
        rows = PARTS[p][2]
        for i, k in enumerate(ks):
            prod[place_of(p, done, group, k), lanes_of(p)] = block[i * rows : (i + 1) * rows]

    ALL4 = range(4)
    h_copy.wait()
    for half in range(2):
        part = pl.ds(half * 256, 256)
        for i in range(blocks):
            if half == 0:
                o_copies[i].wait()
            block = lax.dot_general(
                o_buf[:, pl.ds(i * o_step, o_step)],
                h_buf[:, part],
                (((0,), (0,)), ((), ())),
                preferred_element_type=jnp.float32,
            )
            prod[pl.ds(i * o_step, o_step), part] = block
            block = tiles(block)
            square = jnp.sum(block * block, axis=0)
            most = jnp.max(jnp.abs(block), axis=0)
            squares[:, part] = square if i == 0 else squares[:, part] + square
            largest[:, part] = most if i == 0 else jnp.maximum(largest[:, part], most)
        if half == 0:
            pl.semaphore_wait(barrier, len(greeted))
        for p in Z[half] + XY[half]:
            rows = PARTS[p][2]
            bound = jnp.maximum(largest[:, lanes_of(p)] * (1.0 / TOP), TINY)
            bounds[p] = bound
            sent, inverse = to_send(bound)
            put_scale((p, 0, 1), sent)
            for g in range(8):
                put((p, 0, 1), g * 4 * rows, own(p, 0, g + 8, ALL4), inverse)
            message((p, 0, 1)).start()

    nt = (((1,), (1,)), ((), ()))

    def gram(a, b):
        return lax.dot_general(a, b, nt, preferred_element_type=jnp.float32)

    x_copy.wait()
    mine = x_buf[pl.ds(pl.multiple_of(core * HALF, HALF), HALF), :]
    gram_x[core] = gram(mine, mine)
    quarter = pl.ds(pl.multiple_of(core * 128, 128), 128)
    gram_x[2, quarter, :] = gram(x_buf[quarter, :], x_buf[pl.ds(HALF, HALF), :])

    def to_core(source, target, n):
        return pltpu.make_async_remote_copy(
            src_ref=source,
            dst_ref=target,
            send_sem=mate_send.at[n],
            recv_sem=mate_recv.at[n],
            device_id=other_core,
            device_id_type=MESH,
        )

    grams_out = [
        to_core(gram_x.at[core], gram_x.at[core], 0),
        to_core(gram_x.at[2, quarter], gram_x.at[2, quarter], 1),
    ]
    for copy in grams_out:
        copy.start()
    attn = squares[...]
    partial = (attn[:, :128] + attn[:, 128:256]) + (attn[:, 256:384] + attn[:, 384:])
    for i in range(2):
        c_copies[i].wait()
        low = c_buf[pl.ds(0, HALF), pl.ds(i * c_step, c_step)]
        high = c_buf[pl.ds(HALF, HALF), pl.ds(i * c_step, c_step)]
        for j, (a, b) in enumerate(((low, low), (high, high), (low, high))):
            block = gram(a, b)
            gram_c[j] = block if i == 0 else gram_c[j] + block
    for copy in grams_out:
        copy.wait()
    both = gram_x[0] * gram_c[0] + gram_x[1] * gram_c[1] + 2.0 * (gram_x[2] * gram_c[2])
    both = jnp.sum(tiles(both), axis=0)
    norm_out[0] = partial + (both[:, :128] + both[:, 128:])
    mate = to_core(norm_out.at[0], norm_mate, 2)
    mate.start()
    mate.wait_recv()
    norm_out[1] = norm_out[0] + norm_mate[...]
    norms[0, chip] = norm_out[1]
    norm_copies = []
    for device, slot in [((me_dp, other_chip), 0)] + [
        ((turned((t,)), to), i + 1) for i, t in enumerate(TURNS) for to in (me_t, other_chip)
    ]:
        n = len(norm_copies)
        norm_copies.append(
            pltpu.make_async_remote_copy(
                src_ref=norm_out.at[1],
                dst_ref=norms.at[slot, chip],
                send_sem=norm_send.at[n],
                recv_sem=norm_recv.at[n],
                device_id=device,
                device_id_type=MESH,
            )
        )
    for copy in norm_copies:
        copy.start()
    for copy in norm_copies:
        copy.wait_recv()
    total = norms[:, 0] + norms[:, 1]
    total = jnp.sum(jnp.sum(total, axis=2, keepdims=True), axis=1, keepdims=True)
    factors = threshold / jnp.maximum(jnp.sqrt(jnp.broadcast_to(total, (7, 8, 128))), threshold)
    weights[...] = factors * factor

    def second(parts):
        kept = []
        for p in parts:
            order, _, rows, _ = PARTS[p]
            came = (p, 0, 1)
            message(came).wait_recv()
            mine = weights[0]
            scale = scale_in(came) * weights[1 + TURNS.index(ORDERS[order][0][0])]
            bound = bounds[p] * mine + scale
            bounds[p] = bound
            sent, inverse = to_send(bound)
            put_scale((p, 1, 1), sent)

            def summed(g, p=p, rows=rows, came=came, mine=mine, scale=scale):
                block = flat(tiles(own(p, 1, g, ALL4)) * mine[None])
                return block + got(came, g * 4 * rows, 4 * rows, scale)

            for g in range(4):
                put((p, 1, 1), g * 4 * rows, summed(g + 4), inverse)
            message((p, 1, 1)).start()
            kept.append((p, summed))
        for p, summed in kept:
            for g in range(4):
                keep(p, 1, g, ALL4, summed(g))

    def third(parts):
        kept = []
        for p in parts:
            rows = PARTS[p][2]
            came = (p, 1, 1)
            message(came).wait_recv()
            scale = scale_in(came)
            bound = bounds[p] + scale
            bounds[p] = bound
            sent, inverse = to_send(bound)

            def summed(g, p=p, rows=rows, came=came, scale=scale):
                return own(p, 2, g, ALL4) + got(came, g * 4 * rows, 4 * rows, scale)

            for tau in range(1, 4):
                put_scale((p, 2, tau), sent)
                put((p, 2, tau), 0, summed(tau), inverse)
                message((p, 2, tau)).start()
            kept.append((p, summed))
        for p, summed in kept:
            keep(p, 2, 0, ALL4, summed(0))

    def fourth(half):
        scales, bound = {}, None
        for p in XY[half]:
            here = bounds[p]
            for tau in range(1, 4):
                message((p, 2, tau)).wait_recv()
                scales[p, tau] = scale_in((p, 2, tau))
                here = here + scales[p, tau]
            bound = here if bound is None else jnp.maximum(bound, here)
        sent, inverse = to_send(bound)

        def summed(p, k):
            rows = PARTS[p][2]
            block = own(p, 3, 0, (k,))
            for tau in range(1, 4):
                block = block + got_within((p, 2, tau), k * rows, rows, scales[p, tau])
            return block

        for k in range(1, 4):
            key = ("xy", half, k)
            put_scale(key, sent)
            put(key, 0, jnp.concatenate([summed(p, k) for p in XY[half]], axis=0), inverse)
            message(key).start()
        for p in XY[half]:
            keep(p, 3, 0, (0,), summed(p, 0))

    def third_z():
        scales, bound = {}, None
        for p in Z_ALL:
            message((p, 1, 1)).wait_recv()
            scales[p] = scale_in((p, 1, 1))
            here = bounds[p] + scales[p]
            bound = here if bound is None else jnp.maximum(bound, here)
        sent, inverse = to_send(bound)

        def summed(p, g, ks):
            rows = PARTS[p][2]
            return own(p, 2, g, ks) + got((p, 1, 1), g * 4 * rows + ks[0] * rows, len(ks) * rows, scales[p])

        for owner in range(1, 16):
            key = ("z", 0, owner)
            put_scale(key, sent)
            put(
                key,
                0,
                jnp.concatenate([summed(p, owner // 4, (owner % 4,)) for p in Z_ALL], axis=0),
                inverse,
            )
            message(key).start()
        for p in Z_ALL:
            keep(p, 2, 0, (0,), summed(p, 0, (0,)))

    def finish(parts, kind, half, count):
        done = len(ORDERS[PARTS[parts[0]][0]])
        block = jnp.concatenate([own(p, done, 0, (0,)) for p in parts], axis=0)
        for tau in range(1, count):
            key = (kind, half, tau)
            message(key).wait_recv()
            block = block + got(key, 0, block.shape[0], scale_in(key))
        row = 0
        for p in parts:
            _, first_row, rows, _ = PARTS[p]
            grad[pl.ds(first_row, rows), lanes_of(p)] = block[row : row + rows]
            row += rows

    second(XY[0])
    second(XY[1])
    second(Z_ALL)
    third(XY[0])
    third(XY[1])
    fourth(0)
    third_z()
    fourth(1)
    finish(XY[0], "xy", 0, 4)
    finish(Z_ALL, "z", 0, 16)
    finish(XY[1], "xy", 1, 4)
    clip[0] = factors[0, 0, 0]
    for key in MESSAGES:
        message(key).wait_send()
    for copy in [mate, *norm_copies]:
        copy.wait_send()


def on_device(mlp_input, mlp_cotangent, head_outputs, out_cotangent):
    threshold = 0.5 * SEQ * math.sqrt(D * FF + 4 * HD * D)
    factor = math.sqrt(D * HD / EXAMPLES) / threshold
    f32, bf16 = jnp.float32, jnp.bfloat16
    dma = pltpu.SemaphoreType.DMA
    return pl.pallas_call(
        functools.partial(kernel, threshold, factor),
        out_shape=(
            jax.ShapeDtypeStruct((OWNED, COLS), f32),
            jax.ShapeDtypeStruct((1,), f32),
        ),
        in_specs=[pl.BlockSpec(memory_space=pl.ANY)] * 4,
        out_specs=(
            pl.BlockSpec(memory_space=pltpu.VMEM),
            pl.BlockSpec(memory_space=pltpu.SMEM),
        ),
        scratch_shapes=[
            pltpu.VMEM((SEQ, D), bf16),
            pltpu.VMEM((SEQ, FF // 4), bf16),
            pltpu.VMEM((SEQ, COLS), bf16),
            pltpu.VMEM((SEQ, D), bf16),
            pltpu.VMEM((D, COLS), f32),
            pltpu.VMEM((3, HALF, HALF), f32),
            pltpu.VMEM((3, HALF, HALF), f32),
            pltpu.VMEM((8, COLS), f32),
            pltpu.VMEM((8, COLS), f32),
            pltpu.VMEM((len(PARTS), 8, LANES), f32),
            pltpu.VMEM((MESSAGE_ROWS, LANES), bf16),
            pltpu.VMEM((MESSAGE_ROWS, LANES), bf16),
            pltpu.VMEM((2, 8, LANES), f32),
            pltpu.VMEM((8, LANES), f32),
            pltpu.VMEM((7, 2, 8, LANES), f32),
            pltpu.VMEM((7, 8, LANES), f32),
            dma((2,)),
            dma((3,)),
            dma((2,)),
            dma((len(MESSAGES),)),
            dma((len(MESSAGES),)),
            dma((3,)),
            dma((3,)),
            dma((13,)),
            dma((13,)),
        ],
        compiler_params=pltpu.CompilerParams(
            collective_id=0,
            has_side_effects=True,
            vmem_limit_bytes=56 * 2**20,
        ),
    )(mlp_input, mlp_cotangent, head_outputs, out_cotangent)


def solution(mesh):
    return jax.shard_map(
        on_device,
        mesh=mesh,
        in_specs=(
            P("dp", None, None),
            P("dp", None, "tensor"),
            P("dp", None, "tensor"),
            P("dp", None, None),
        ),
        out_specs=(P("dp", "tensor"), P("dp")),
        check_vma=False,
    )
```

```python
import functools
import itertools
import math

import jax
import jax.numpy as jnp
from jax import lax
from jax.experimental import pallas as pl
from jax.experimental.pallas import tpu as pltpu
from jax.sharding import PartitionSpec as P

D = 4608
FF = 36864
HD = 2048
SEQ = 512
EXAMPLES = 64
OWNED = D // EXAMPLES
COLS = 512
LANES = 128
HALF = SEQ // 2
MESH = pl.DeviceIdType.MESH

X0, X1, Y0, Y1, Z0, Z1 = (0, 0), (0, 1), (1, 0), (1, 1), (2, 0), (2, 1)
TURNS = (X0, X1, Y0, Y1, Z0, Z1)
ALONG_Z = (Z0, Z1)
PLANE = (X0, X1, Y0, Y1)
ORDERS = (
    ((X0,), (Y0,), (X1, Y1), ALONG_Z),
    ((Y0,), (X1,), (Y1, X0), ALONG_Z),
    ((X1,), (Y1,), (X0, Y0), ALONG_Z),
    ((Y1,), (X0,), (Y0, X1), ALONG_Z),
    ((Z0,), (Z1,), PLANE),
    ((Z1,), (Z0,), PLANE),
)
PARTS = (
    (0, 0, 32, 0),
    (1, 32, 24, 0),
    (2, 0, 32, 1),
    (3, 32, 24, 1),
    (4, 56, 16, 0),
    (5, 56, 16, 1),
    (1, 0, 32, 2),
    (0, 32, 24, 2),
    (3, 0, 32, 3),
    (2, 32, 24, 3),
    (4, 56, 16, 2),
    (5, 56, 16, 3),
)
XY = ((0, 1, 2, 3), (6, 7, 8, 9))
Z = ((4, 5), (10, 11))
Z_ALL = Z[0] + Z[1]
SCALE_ROWS = 16
POWER = 12
TOP = 1400.0
UP = 1.004
TINY = 1e-30


def layout():
    table, row = {}, 0

    def add(key, rows, turns):
        nonlocal row
        table[key] = (row, rows, turns)
        row += rows + SCALE_ROWS

    def reached(turns):
        for tau in range(1, 1 << len(turns)):
            bits = [(tau >> (len(turns) - 1 - i)) & 1 for i in range(len(turns))]
            yield tau, tuple(t for t, b in zip(turns, bits) if b)

    for p, (order, _, rows, _) in enumerate(PARTS):
        steps = ORDERS[order]
        add((p, 0, 1), 32 * rows, steps[0])
        add((p, 1, 1), 16 * rows, steps[1])
        if len(steps) == 4:
            for tau, turns in reached(steps[2]):
                add((p, 2, tau), 4 * rows, turns)
    for half in range(2):
        for tau, turns in reached(ALONG_Z):
            add(("xy", half, tau), sum(PARTS[p][2] for p in XY[half]), turns)
    for tau, turns in reached(PLANE):
        add(("z", 0, tau), sum(PARTS[p][2] for p in Z_ALL), turns)
    return table, row


MESSAGES, MESSAGE_ROWS = layout()
NUMBER = {key: i for i, key in enumerate(MESSAGES)}


def turn(v, kind, bit):
    step = 1 - 2 * lax.rem(v, 2) if kind == 0 else 3 - 2 * v
    return v + bit * step


def tiles(block):
    return block.reshape(block.shape[0] // 8, 8, block.shape[1])


def flat(block):
    return block.reshape(block.shape[0] * 8, block.shape[2])


def encode(block, inverse):
    v = tiles(block) * inverse[None]
    v2 = v * v
    v4 = v2 * v2
    power = v4 * v4 * v4
    return flat(jnp.where(v < 0, -power, power)).astype(jnp.bfloat16)


def decode(power, scale):
    v = jnp.exp2(jnp.log2(jnp.abs(power)) * (1.0 / POWER))
    return flat(tiles(jnp.where(power < 0, -v, v)) * scale[None])


def kernel(
    threshold,
    factor,
    mlp_in,
    mlp_cot,
    heads_in,
    out_cot,
    grad,
    clip,
    x_buf,
    c_buf,
    h_buf,
    o_buf,
    prod_a,
    prod_b,
    gram_x,
    gram_c,
    squares,
    largest,
    bounds,
    outgoing,
    incoming,
    norm_out,
    norm_mate,
    norms,
    weights,
    in_sem,
    o_sem,
    c_sem,
    send_sem,
    recv_sem,
    mate_send,
    mate_recv,
    norm_send,
    norm_recv,
):
    me_dp = lax.axis_index("dp")
    me_t = lax.axis_index("tensor")
    core = lax.rem(me_t, 2)
    chip = lax.div(me_t, 2)
    place = (lax.div(me_dp, 16), lax.rem(lax.div(me_dp, 4), 4), lax.rem(me_dp, 4))

    def index_of(at):
        return at[0] * 16 + at[1] * 4 + at[2]

    def turned(turns):
        at = list(place)
        for axis, kind in turns:
            at[axis] = turn(at[axis], kind, 1)
        return index_of(at)

    o_step, c_step = 1536, D
    blocks = D // o_step

    def columns(source, target, start, size, sem):
        return pltpu.make_async_copy(
            source.at[0, :, pl.ds(start, size)], target.at[:, pl.ds(start, size)], sem
        )

    h_copy = pltpu.make_async_copy(heads_in.at[0], h_buf, in_sem.at[0])
    x_copy = pltpu.make_async_copy(mlp_in.at[0], x_buf, in_sem.at[1])
    o_copies = [columns(out_cot, o_buf, i * o_step, o_step, o_sem.at[i]) for i in range(blocks)]
    c_copies = [columns(mlp_cot, c_buf, i * c_step, c_step, c_sem.at[i]) for i in range(2)]
    for copy in [h_copy, *o_copies, x_copy, *c_copies]:
        copy.start()

    barrier = pltpu.get_barrier_semaphore()
    other_chip = lax.rem(me_t + 2, 4)
    other_core = (me_dp, turn(me_t, 0, 1))
    subsets = [s for n in range(1, 5) for s in itertools.combinations(PLANE, n)]
    subsets += [(Z0,), (Z1,), ALONG_Z]
    greeted = [(turned(s), me_t) for s in subsets]
    greeted += [(turned((t,)), other_chip) for t in TURNS]
    greeted += [(me_dp, other_chip), other_core]
    for device in greeted:
        pl.semaphore_signal(barrier, inc=1, device_id=device, device_id_type=MESH)

    def rows_of_message(key, ref):
        start, rows, _ = MESSAGES[key]
        return ref.at[pl.ds(start, rows + SCALE_ROWS)]

    def message(key):
        n = NUMBER[key]
        return pltpu.make_async_remote_copy(
            src_ref=rows_of_message(key, outgoing),
            dst_ref=rows_of_message(key, incoming),
            send_sem=send_sem.at[n],
            recv_sem=recv_sem.at[n],
            device_id=(turned(MESSAGES[key][2]), me_t),
            device_id_type=MESH,
        )

    def put_scale(key, sent):
        start, rows, _ = MESSAGES[key]
        outgoing[pl.ds(start + rows, SCALE_ROWS), :] = jnp.concatenate([sent, sent], axis=0)

    def put(key, at, block, inverse):
        outgoing[pl.ds(MESSAGES[key][0] + at, block.shape[0]), :] = encode(block, inverse)

    def scale_in(key):
        start, rows, _ = MESSAGES[key]
        return incoming[pl.ds(start + rows, SCALE_ROWS), :].astype(jnp.float32)[:8]

    def got(key, at, size, scale):
        return decode(incoming[pl.ds(MESSAGES[key][0] + at, size), :].astype(jnp.float32), scale)

    def got_within(key, at, size, scale):
        low, high = at // 16 * 16, -(-(at + size) // 16) * 16
        raw = incoming[pl.ds(MESSAGES[key][0] + low, high - low), :].astype(jnp.float32)
        return decode(raw[at - low : at - low + size], scale)

    def to_send(bound):
        sent = (bound * UP).astype(jnp.bfloat16)
        return sent, 1.0 / sent.astype(jnp.float32)

    prods = (prod_a, prod_b)

    def lanes_of(p):
        return pl.ds(PARTS[p][3] * LANES, LANES)

    def held(p):
        return prods[PARTS[p][3] // 2], pl.ds(PARTS[p][3] % 2 * LANES, LANES)

    bases = {}
    for axis, stride in enumerate((16 * OWNED, 4 * OWNED, OWNED)):
        for zero in range(2):
            for one in range(2):
                at = place[axis]
                if zero:
                    at = turn(at, 0, 1)
                if one:
                    at = turn(at, 1, 1)
                bases[axis, zero, one] = at * stride

    def place_of(p, done, group, k):
        order = list(itertools.chain(*ORDERS[PARTS[p][0]][done:]))
        owner = 4 * group + k
        bits = {t: (owner >> (len(order) - 1 - i)) & 1 for i, t in enumerate(order)}
        start = PARTS[p][1] + sum(bases[a, bits.get((a, 0), 0), bits.get((a, 1), 0)] for a in range(3))
        return pl.ds(pl.multiple_of(start, 8), PARTS[p][2])

    def own(p, done, group, ks):
        ref, lanes = held(p)
        return jnp.concatenate([ref[place_of(p, done, group, k), lanes] for k in ks], axis=0)

    def keep(p, done, group, ks, block):
        rows = PARTS[p][2]
        ref, lanes = held(p)
        for i, k in enumerate(ks):
            ref[place_of(p, done, group, k), lanes] = block[i * rows : (i + 1) * rows]

    ALL4 = range(4)

    def first(half):
        for p in Z[half] + XY[half]:
            rows = PARTS[p][2]
            bound = jnp.maximum(largest[:, lanes_of(p)] * (1.0 / TOP), TINY)
            bounds[p] = bound
            sent, inverse = to_send(bound)
            put_scale((p, 0, 1), sent)
            for g in range(8):
                put((p, 0, 1), g * 4 * rows, own(p, 0, g + 8, ALL4), inverse)
            message((p, 0, 1)).start()

    h_copy.wait()
    for half in range(2):
        part = pl.ds(half * 256, 256)
        for i in range(blocks):
            if half == 0:
                o_copies[i].wait()
            block = lax.dot_general(
                o_buf[:, pl.ds(i * o_step, o_step)],
                h_buf[:, part],
                (((0,), (0,)), ((), ())),
                preferred_element_type=jnp.float32,
            )
            prods[half][pl.ds(i * o_step, o_step), :] = block
            block = tiles(block)
            square = jnp.sum(block * block, axis=0)
            most = jnp.max(jnp.abs(block), axis=0)
            squares[:, part] = square if i == 0 else squares[:, part] + square
            largest[:, part] = most if i == 0 else jnp.maximum(largest[:, part], most)
        if half == 0:
            pl.semaphore_wait(barrier, len(greeted))
        if half == 0:
            first(0)

    nt = (((1,), (1,)), ((), ()))

    def gram(a, b):
        return lax.dot_general(a, b, nt, preferred_element_type=jnp.float32)

    x_copy.wait()
    mine = x_buf[pl.ds(pl.multiple_of(core * HALF, HALF), HALF), :]
    gram_x[core] = gram(mine, mine)
    quarter = pl.ds(pl.multiple_of(core * 128, 128), 128)
    gram_x[2, quarter, :] = gram(x_buf[quarter, :], x_buf[pl.ds(HALF, HALF), :])

    def to_core(source, target, n):
        return pltpu.make_async_remote_copy(
            src_ref=source,
            dst_ref=target,
            send_sem=mate_send.at[n],
            recv_sem=mate_recv.at[n],
            device_id=other_core,
            device_id_type=MESH,
        )

    grams_out = [
        to_core(gram_x.at[core], gram_x.at[core], 0),
        to_core(gram_x.at[2, quarter], gram_x.at[2, quarter], 1),
    ]
    for copy in grams_out:
        copy.start()
    attn = squares[...]
    partial = (attn[:, :128] + attn[:, 128:256]) + (attn[:, 256:384] + attn[:, 384:])
    for i in range(2):
        c_copies[i].wait()
        low = c_buf[pl.ds(0, HALF), pl.ds(i * c_step, c_step)]
        high = c_buf[pl.ds(HALF, HALF), pl.ds(i * c_step, c_step)]
        for j, (a, b) in enumerate(((low, low), (high, high), (low, high))):
            block = gram(a, b)
            gram_c[j] = block if i == 0 else gram_c[j] + block
    for copy in grams_out:
        copy.wait()
    both = gram_x[0] * gram_c[0] + gram_x[1] * gram_c[1] + 2.0 * (gram_x[2] * gram_c[2])
    both = jnp.sum(tiles(both), axis=0)
    norm_out[0] = partial + (both[:, :128] + both[:, 128:])
    mate = to_core(norm_out.at[0], norm_mate, 2)
    mate.start()
    mate.wait_recv()
    norm_out[1] = norm_out[0] + norm_mate[...]
    norms[0, chip] = norm_out[1]
    norm_copies = []
    for device, slot in [((me_dp, other_chip), 0)] + [
        ((turned((t,)), to), i + 1) for i, t in enumerate(TURNS) for to in (me_t, other_chip)
    ]:
        n = len(norm_copies)
        norm_copies.append(
            pltpu.make_async_remote_copy(
                src_ref=norm_out.at[1],
                dst_ref=norms.at[slot, chip],
                send_sem=norm_send.at[n],
                recv_sem=norm_recv.at[n],
                device_id=device,
                device_id_type=MESH,
            )
        )
    for copy in norm_copies:
        copy.start()
    first(1)
    for copy in norm_copies:
        copy.wait_recv()
    total = norms[:, 0] + norms[:, 1]
    total = jnp.sum(jnp.sum(total, axis=2, keepdims=True), axis=1, keepdims=True)
    factors = threshold / jnp.maximum(jnp.sqrt(jnp.broadcast_to(total, (7, 8, 128))), threshold)
    weights[...] = factors * factor

    def second(parts):
        kept = []
        for p in parts:
            order, _, rows, _ = PARTS[p]
            came = (p, 0, 1)
            message(came).wait_recv()
            mine = weights[0]
            scale = scale_in(came) * weights[1 + TURNS.index(ORDERS[order][0][0])]
            bound = bounds[p] * mine + scale
            bounds[p] = bound
            sent, inverse = to_send(bound)
            put_scale((p, 1, 1), sent)

            def summed(g, p=p, rows=rows, came=came, mine=mine, scale=scale):
                block = flat(tiles(own(p, 1, g, ALL4)) * mine[None])
                return block + got(came, g * 4 * rows, 4 * rows, scale)

            for g in range(4):
                put((p, 1, 1), g * 4 * rows, summed(g + 4), inverse)
            message((p, 1, 1)).start()
            kept.append((p, summed))
        for p, summed in kept:
            for g in range(4):
                keep(p, 1, g, ALL4, summed(g))

    def third(parts):
        kept = []
        for p in parts:
            rows = PARTS[p][2]
            came = (p, 1, 1)
            message(came).wait_recv()
            scale = scale_in(came)
            bound = bounds[p] + scale
            bounds[p] = bound
            sent, inverse = to_send(bound)

            def summed(g, p=p, rows=rows, came=came, scale=scale):
                return own(p, 2, g, ALL4) + got(came, g * 4 * rows, 4 * rows, scale)

            for tau in range(1, 4):
                put_scale((p, 2, tau), sent)
                put((p, 2, tau), 0, summed(tau), inverse)
                message((p, 2, tau)).start()
            kept.append((p, summed))
        for p, summed in kept:
            keep(p, 2, 0, ALL4, summed(0))

    def fourth(half):
        scales, bound = {}, None
        for p in XY[half]:
            here = bounds[p]
            for tau in range(1, 4):
                message((p, 2, tau)).wait_recv()
                scales[p, tau] = scale_in((p, 2, tau))
                here = here + scales[p, tau]
            bound = here if bound is None else jnp.maximum(bound, here)
        sent, inverse = to_send(bound)

        def summed(p, k):
            rows = PARTS[p][2]
            block = own(p, 3, 0, (k,))
            for tau in range(1, 4):
                block = block + got_within((p, 2, tau), k * rows, rows, scales[p, tau])
            return block

        for k in range(1, 4):
            key = ("xy", half, k)
            put_scale(key, sent)
            put(key, 0, jnp.concatenate([summed(p, k) for p in XY[half]], axis=0), inverse)
            message(key).start()
        for p in XY[half]:
            keep(p, 3, 0, (0,), summed(p, 0))

    def third_z():
        scales, bound = {}, None
        for p in Z_ALL:
            message((p, 1, 1)).wait_recv()
            scales[p] = scale_in((p, 1, 1))
            here = bounds[p] + scales[p]
            bound = here if bound is None else jnp.maximum(bound, here)
        sent, inverse = to_send(bound)

        def summed(p, g, ks):
            rows = PARTS[p][2]
            return own(p, 2, g, ks) + got((p, 1, 1), g * 4 * rows + ks[0] * rows, len(ks) * rows, scales[p])

        for owner in range(1, 16):
            key = ("z", 0, owner)
            put_scale(key, sent)
            put(
                key,
                0,
                jnp.concatenate([summed(p, owner // 4, (owner % 4,)) for p in Z_ALL], axis=0),
                inverse,
            )
            message(key).start()
        for p in Z_ALL:
            keep(p, 2, 0, (0,), summed(p, 0, (0,)))

    def finish(parts, kind, half, count):
        done = len(ORDERS[PARTS[parts[0]][0]])
        block = jnp.concatenate([own(p, done, 0, (0,)) for p in parts], axis=0)
        for tau in range(1, count):
            key = (kind, half, tau)
            message(key).wait_recv()
            block = block + got(key, 0, block.shape[0], scale_in(key))
        row = 0
        for p in parts:
            _, first_row, rows, _ = PARTS[p]
            grad[pl.ds(first_row, rows), lanes_of(p)] = block[row : row + rows]
            row += rows

    second(XY[0])
    second(XY[1])
    second(Z_ALL)
    third(XY[0])
    third(XY[1])
    fourth(0)
    third_z()
    fourth(1)
    finish(XY[0], "xy", 0, 4)
    finish(Z_ALL, "z", 0, 16)
    finish(XY[1], "xy", 1, 4)
    clip[0] = factors[0, 0, 0]
    for key in MESSAGES:
        message(key).wait_send()
    for copy in [mate, *norm_copies]:
        copy.wait_send()


def on_device(mlp_input, mlp_cotangent, head_outputs, out_cotangent):
    threshold = 0.5 * SEQ * math.sqrt(D * FF + 4 * HD * D)
    factor = math.sqrt(D * HD / EXAMPLES) / threshold
    f32, bf16 = jnp.float32, jnp.bfloat16
    dma = pltpu.SemaphoreType.DMA
    return pl.pallas_call(
        functools.partial(kernel, threshold, factor),
        out_shape=(
            jax.ShapeDtypeStruct((OWNED, COLS), f32),
            jax.ShapeDtypeStruct((1,), f32),
        ),
        in_specs=[pl.BlockSpec(memory_space=pl.ANY)] * 4,
        out_specs=(
            pl.BlockSpec(memory_space=pltpu.VMEM),
            pl.BlockSpec(memory_space=pltpu.SMEM),
        ),
        scratch_shapes=[
            pltpu.VMEM((SEQ, D), bf16),
            pltpu.VMEM((SEQ, FF // 4), bf16),
            pltpu.VMEM((SEQ, COLS), bf16),
            pltpu.VMEM((SEQ, D), bf16),
            pltpu.VMEM((D, 256), f32),
            pltpu.VMEM((D, 256), f32),
            pltpu.VMEM((3, HALF, HALF), f32),
            pltpu.VMEM((3, HALF, HALF), f32),
            pltpu.VMEM((8, COLS), f32),
            pltpu.VMEM((8, COLS), f32),
            pltpu.VMEM((len(PARTS), 8, LANES), f32),
            pltpu.VMEM((MESSAGE_ROWS, LANES), bf16),
            pltpu.VMEM((MESSAGE_ROWS, LANES), bf16),
            pltpu.VMEM((2, 8, LANES), f32),
            pltpu.VMEM((8, LANES), f32),
            pltpu.VMEM((7, 2, 8, LANES), f32),
            pltpu.VMEM((7, 8, LANES), f32),
            dma((2,)),
            dma((3,)),
            dma((2,)),
            dma((len(MESSAGES),)),
            dma((len(MESSAGES),)),
            dma((3,)),
            dma((3,)),
            dma((13,)),
            dma((13,)),
        ],
        compiler_params=pltpu.CompilerParams(
            collective_id=0,
            has_side_effects=True,
            vmem_limit_bytes=56 * 2**20,
        ),
    )(mlp_input, mlp_cotangent, head_outputs, out_cotangent)


def solution(mesh):
    return jax.shard_map(
        on_device,
        mesh=mesh,
        in_specs=(
            P("dp", None, None),
            P("dp", None, "tensor"),
            P("dp", None, "tensor"),
            P("dp", None, None),
        ),
        out_specs=(P("dp", "tensor"), P("dp")),
        check_vma=False,
    )
```

```python
import functools
import itertools
import math

import jax
import jax.numpy as jnp
from jax import lax
from jax.experimental import pallas as pl
from jax.experimental.pallas import tpu as pltpu
from jax.sharding import PartitionSpec as P

D = 4608
FF = 36864
HD = 2048
SEQ = 512
EXAMPLES = 64
OWNED = D // EXAMPLES
COLS = 512
LANES = 128
HALF = SEQ // 2
MESH = pl.DeviceIdType.MESH

X0, X1, Y0, Y1, Z0, Z1 = (0, 0), (0, 1), (1, 0), (1, 1), (2, 0), (2, 1)
TURNS = (X0, X1, Y0, Y1, Z0, Z1)
ALONG_Z = (Z0, Z1)
PLANE = (X0, X1, Y0, Y1)
ORDERS = (
    ((X0,), (Y0,), (X1, Y1), ALONG_Z),
    ((Y0,), (X1,), (Y1, X0), ALONG_Z),
    ((X1,), (Y1,), (X0, Y0), ALONG_Z),
    ((Y1,), (X0,), (Y0, X1), ALONG_Z),
    ((Z0,), (Z1,), PLANE),
    ((Z1,), (Z0,), PLANE),
)
PARTS = (
    (0, 0, 32, 0),
    (1, 32, 24, 0),
    (2, 0, 32, 1),
    (3, 32, 24, 1),
    (4, 56, 16, 0),
    (5, 56, 16, 1),
    (1, 0, 32, 2),
    (0, 32, 24, 2),
    (3, 0, 32, 3),
    (2, 32, 24, 3),
    (4, 56, 16, 2),
    (5, 56, 16, 3),
)
XY = ((0, 1, 2, 3), (6, 7, 8, 9))
Z = ((4, 5), (10, 11))
Z_ALL = Z[0] + Z[1]
SCALE_ROWS = 16
POWER = 12
TOP = 1400.0
UP = 1.004
TINY = 1e-30


def layout():
    table, row = {}, 0

    def add(key, rows, turns):
        nonlocal row
        table[key] = (row, rows, turns)
        row += rows + SCALE_ROWS

    def reached(turns):
        for tau in range(1, 1 << len(turns)):
            bits = [(tau >> (len(turns) - 1 - i)) & 1 for i in range(len(turns))]
            yield tau, tuple(t for t, b in zip(turns, bits) if b)

    for p, (order, _, rows, _) in enumerate(PARTS):
        steps = ORDERS[order]
        add((p, 0, 1), 32 * rows, steps[0])
        add((p, 1, 1), 16 * rows, steps[1])
        if len(steps) == 4:
            for tau, turns in reached(steps[2]):
                add((p, 2, tau), 4 * rows, turns)
    for half in range(2):
        for tau, turns in reached(ALONG_Z):
            add(("xy", half, tau), sum(PARTS[p][2] for p in XY[half]), turns)
    for tau, turns in reached(PLANE):
        add(("z", 0, tau), sum(PARTS[p][2] for p in Z_ALL), turns)
    return table, row


MESSAGES, MESSAGE_ROWS = layout()
NUMBER = {key: i for i, key in enumerate(MESSAGES)}


def turn(v, kind, bit):
    step = 1 - 2 * lax.rem(v, 2) if kind == 0 else 3 - 2 * v
    return v + bit * step


def tiles(block):
    return block.reshape(block.shape[0] // 8, 8, block.shape[1])


def flat(block):
    return block.reshape(block.shape[0] * 8, block.shape[2])


def encode(block, inverse):
    v = tiles(block) * inverse[None]
    v2 = v * v
    v4 = v2 * v2
    power = v4 * v4 * v4
    return flat(jnp.where(v < 0, -power, power)).astype(jnp.bfloat16)


def decode(power, scale):
    v = jnp.exp2(jnp.log2(jnp.abs(power)) * (1.0 / POWER))
    return flat(tiles(jnp.where(power < 0, -v, v)) * scale[None])


def kernel(
    threshold,
    factor,
    mlp_in,
    mlp_cot,
    heads_in,
    out_cot,
    grad,
    clip,
    x_buf,
    c_buf,
    h_buf,
    o_buf,
    prod_a,
    prod_b,
    gram_x,
    gram_c,
    squares,
    largest,
    bounds,
    outgoing,
    incoming,
    norm_out,
    norm_mate,
    norms,
    weights,
    in_sem,
    o_sem,
    c_sem,
    send_sem,
    recv_sem,
    mate_send,
    mate_recv,
    norm_send,
    norm_recv,
):
    me_dp = lax.axis_index("dp")
    me_t = lax.axis_index("tensor")
    core = lax.rem(me_t, 2)
    chip = lax.div(me_t, 2)
    place = (lax.div(me_dp, 16), lax.rem(lax.div(me_dp, 4), 4), lax.rem(me_dp, 4))

    def index_of(at):
        return at[0] * 16 + at[1] * 4 + at[2]

    def turned(turns):
        at = list(place)
        for axis, kind in turns:
            at[axis] = turn(at[axis], kind, 1)
        return index_of(at)

    o_step, c_step = 1536, D
    blocks = D // o_step

    def columns(source, target, start, size, sem):
        return pltpu.make_async_copy(
            source.at[0, :, pl.ds(start, size)], target.at[:, pl.ds(start, size)], sem
        )

    h_copy = pltpu.make_async_copy(heads_in.at[0], h_buf, in_sem.at[0])
    x_copy = pltpu.make_async_copy(mlp_in.at[0], x_buf, in_sem.at[1])
    o_copies = [columns(out_cot, o_buf, i * o_step, o_step, o_sem.at[i]) for i in range(blocks)]
    c_copies = [columns(mlp_cot, c_buf, i * c_step, c_step, c_sem.at[i]) for i in range(2)]
    for copy in [h_copy, *o_copies, x_copy, *c_copies]:
        copy.start()

    barrier = pltpu.get_barrier_semaphore()
    other_chip = lax.rem(me_t + 2, 4)
    other_core = (me_dp, turn(me_t, 0, 1))
    subsets = [s for n in range(1, 5) for s in itertools.combinations(PLANE, n)]
    subsets += [(Z0,), (Z1,), ALONG_Z]
    greeted = [(turned(s), me_t) for s in subsets]
    greeted += [(turned((t,)), other_chip) for t in TURNS]
    greeted += [(me_dp, other_chip), other_core]
    for device in greeted:
        pl.semaphore_signal(barrier, inc=1, device_id=device, device_id_type=MESH)

    def rows_of_message(key, ref):
        start, rows, _ = MESSAGES[key]
        return ref.at[pl.ds(start, rows + SCALE_ROWS)]

    def message(key):
        n = NUMBER[key]
        return pltpu.make_async_remote_copy(
            src_ref=rows_of_message(key, outgoing),
            dst_ref=rows_of_message(key, incoming),
            send_sem=send_sem.at[n],
            recv_sem=recv_sem.at[n],
            device_id=(turned(MESSAGES[key][2]), me_t),
            device_id_type=MESH,
        )

    def put_scale(key, sent):
        start, rows, _ = MESSAGES[key]
        outgoing[pl.ds(start + rows, SCALE_ROWS), :] = jnp.concatenate([sent, sent], axis=0)

    def put(key, at, block, inverse):
        outgoing[pl.ds(MESSAGES[key][0] + at, block.shape[0]), :] = encode(block, inverse)

    def scale_in(key):
        start, rows, _ = MESSAGES[key]
        return incoming[pl.ds(start + rows, SCALE_ROWS), :].astype(jnp.float32)[:8]

    def got(key, at, size, scale):
        return decode(incoming[pl.ds(MESSAGES[key][0] + at, size), :].astype(jnp.float32), scale)

    def got_within(key, at, size, scale):
        low, high = at // 16 * 16, -(-(at + size) // 16) * 16
        raw = incoming[pl.ds(MESSAGES[key][0] + low, high - low), :].astype(jnp.float32)
        return decode(raw[at - low : at - low + size], scale)

    def to_send(bound):
        sent = (bound * UP).astype(jnp.bfloat16)
        return sent, 1.0 / sent.astype(jnp.float32)

    prods = (prod_a, prod_b)

    def lanes_of(p):
        return pl.ds(PARTS[p][3] * LANES, LANES)

    def held(p):
        return prods[PARTS[p][3] // 2], pl.ds(PARTS[p][3] % 2 * LANES, LANES)

    bases = {}
    for axis, stride in enumerate((16 * OWNED, 4 * OWNED, OWNED)):
        for zero in range(2):
            for one in range(2):
                at = place[axis]
                if zero:
                    at = turn(at, 0, 1)
                if one:
                    at = turn(at, 1, 1)
                bases[axis, zero, one] = at * stride

    def place_of(p, done, group, k):
        order = list(itertools.chain(*ORDERS[PARTS[p][0]][done:]))
        owner = 4 * group + k
        bits = {t: (owner >> (len(order) - 1 - i)) & 1 for i, t in enumerate(order)}
        start = PARTS[p][1] + sum(bases[a, bits.get((a, 0), 0), bits.get((a, 1), 0)] for a in range(3))
        return pl.ds(pl.multiple_of(start, 8), PARTS[p][2])

    def own(p, done, group, ks):
        ref, lanes = held(p)
        return jnp.concatenate([ref[place_of(p, done, group, k), lanes] for k in ks], axis=0)

    def keep(p, done, group, ks, block):
        rows = PARTS[p][2]
        ref, lanes = held(p)
        for i, k in enumerate(ks):
            ref[place_of(p, done, group, k), lanes] = block[i * rows : (i + 1) * rows]

    ALL4 = range(4)

    def first(parts):
        for p in parts:
            rows = PARTS[p][2]
            bound = jnp.maximum(largest[:, lanes_of(p)] * (1.0 / TOP), TINY)
            bounds[p] = bound
            sent, inverse = to_send(bound)
            put_scale((p, 0, 1), sent)
            for g in range(8):
                put((p, 0, 1), g * 4 * rows, own(p, 0, g + 8, ALL4), inverse)
            message((p, 0, 1)).start()

    h_copy.wait()
    for half in range(2):
        part = pl.ds(half * 256, 256)
        for i in range(blocks):
            if half == 0:
                o_copies[i].wait()
            block = lax.dot_general(
                o_buf[:, pl.ds(i * o_step, o_step)],
                h_buf[:, part],
                (((0,), (0,)), ((), ())),
                preferred_element_type=jnp.float32,
            )
            prods[half][pl.ds(i * o_step, o_step), :] = block
            block = tiles(block)
            square = jnp.sum(block * block, axis=0)
            most = jnp.max(jnp.abs(block), axis=0)
            squares[:, part] = square if i == 0 else squares[:, part] + square
            largest[:, part] = most if i == 0 else jnp.maximum(largest[:, part], most)
        if half == 0:
            pl.semaphore_wait(barrier, len(greeted))
        first(Z[0] + XY[0] if half == 0 else Z[1])

    nt = (((1,), (1,)), ((), ()))

    def gram(a, b):
        return lax.dot_general(a, b, nt, preferred_element_type=jnp.float32)

    x_copy.wait()
    mine = x_buf[pl.ds(pl.multiple_of(core * HALF, HALF), HALF), :]
    gram_x[core] = gram(mine, mine)
    quarter = pl.ds(pl.multiple_of(core * 128, 128), 128)
    gram_x[2, quarter, :] = gram(x_buf[quarter, :], x_buf[pl.ds(HALF, HALF), :])

    def to_core(source, target, n):
        return pltpu.make_async_remote_copy(
            src_ref=source,
            dst_ref=target,
            send_sem=mate_send.at[n],
            recv_sem=mate_recv.at[n],
            device_id=other_core,
            device_id_type=MESH,
        )

    grams_out = [
        to_core(gram_x.at[core], gram_x.at[core], 0),
        to_core(gram_x.at[2, quarter], gram_x.at[2, quarter], 1),
    ]
    for copy in grams_out:
        copy.start()
    attn = squares[...]
    partial = (attn[:, :128] + attn[:, 128:256]) + (attn[:, 256:384] + attn[:, 384:])
    for i in range(2):
        c_copies[i].wait()
        low = c_buf[pl.ds(0, HALF), pl.ds(i * c_step, c_step)]
        high = c_buf[pl.ds(HALF, HALF), pl.ds(i * c_step, c_step)]
        for j, (a, b) in enumerate(((low, low), (high, high), (low, high))):
            block = gram(a, b)
            gram_c[j] = block if i == 0 else gram_c[j] + block
    for copy in grams_out:
        copy.wait()
    both = gram_x[0] * gram_c[0] + gram_x[1] * gram_c[1] + 2.0 * (gram_x[2] * gram_c[2])
    both = jnp.sum(tiles(both), axis=0)
    norm_out[0] = partial + (both[:, :128] + both[:, 128:])
    mate = to_core(norm_out.at[0], norm_mate, 2)
    mate.start()
    mate.wait_recv()
    norm_out[1] = norm_out[0] + norm_mate[...]
    norms[0, chip] = norm_out[1]
    norm_copies = []
    for device, slot in [((me_dp, other_chip), 0)] + [
        ((turned((t,)), to), i + 1) for i, t in enumerate(TURNS) for to in (me_t, other_chip)
    ]:
        n = len(norm_copies)
        norm_copies.append(
            pltpu.make_async_remote_copy(
                src_ref=norm_out.at[1],
                dst_ref=norms.at[slot, chip],
                send_sem=norm_send.at[n],
                recv_sem=norm_recv.at[n],
                device_id=device,
                device_id_type=MESH,
            )
        )
    for copy in norm_copies:
        copy.start()
    first(XY[1])
    for copy in norm_copies:
        copy.wait_recv()
    total = norms[:, 0] + norms[:, 1]
    total = jnp.sum(jnp.sum(total, axis=2, keepdims=True), axis=1, keepdims=True)
    factors = threshold / jnp.maximum(jnp.sqrt(jnp.broadcast_to(total, (7, 8, 128))), threshold)
    weights[...] = factors * factor

    def second(parts):
        kept = []
        for p in parts:
            order, _, rows, _ = PARTS[p]
            came = (p, 0, 1)
            message(came).wait_recv()
            mine = weights[0]
            scale = scale_in(came) * weights[1 + TURNS.index(ORDERS[order][0][0])]
            bound = bounds[p] * mine + scale
            bounds[p] = bound
            sent, inverse = to_send(bound)
            put_scale((p, 1, 1), sent)

            def summed(g, p=p, rows=rows, came=came, mine=mine, scale=scale):
                block = flat(tiles(own(p, 1, g, ALL4)) * mine[None])
                return block + got(came, g * 4 * rows, 4 * rows, scale)

            for g in range(4):
                put((p, 1, 1), g * 4 * rows, summed(g + 4), inverse)
            message((p, 1, 1)).start()
            kept.append((p, summed))
        for p, summed in kept:
            for g in range(4):
                keep(p, 1, g, ALL4, summed(g))

    def third(parts):
        kept = []
        for p in parts:
            rows = PARTS[p][2]
            came = (p, 1, 1)
            message(came).wait_recv()
            scale = scale_in(came)
            bound = bounds[p] + scale
            bounds[p] = bound
            sent, inverse = to_send(bound)

            def summed(g, p=p, rows=rows, came=came, scale=scale):
                return own(p, 2, g, ALL4) + got(came, g * 4 * rows, 4 * rows, scale)

            for tau in range(1, 4):
                put_scale((p, 2, tau), sent)
                put((p, 2, tau), 0, summed(tau), inverse)
                message((p, 2, tau)).start()
            kept.append((p, summed))
        for p, summed in kept:
            keep(p, 2, 0, ALL4, summed(0))

    def fourth(half):
        scales, bound = {}, None
        for p in XY[half]:
            here = bounds[p]
            for tau in range(1, 4):
                message((p, 2, tau)).wait_recv()
                scales[p, tau] = scale_in((p, 2, tau))
                here = here + scales[p, tau]
            bound = here if bound is None else jnp.maximum(bound, here)
        sent, inverse = to_send(bound)

        def summed(p, k):
            rows = PARTS[p][2]
            block = own(p, 3, 0, (k,))
            for tau in range(1, 4):
                block = block + got_within((p, 2, tau), k * rows, rows, scales[p, tau])
            return block

        for k in range(1, 4):
            key = ("xy", half, k)
            put_scale(key, sent)
            put(key, 0, jnp.concatenate([summed(p, k) for p in XY[half]], axis=0), inverse)
            message(key).start()
        for p in XY[half]:
            keep(p, 3, 0, (0,), summed(p, 0))

    def third_z():
        scales, bound = {}, None
        for p in Z_ALL:
            message((p, 1, 1)).wait_recv()
            scales[p] = scale_in((p, 1, 1))
            here = bounds[p] + scales[p]
            bound = here if bound is None else jnp.maximum(bound, here)
        sent, inverse = to_send(bound)

        def summed(p, g, ks):
            rows = PARTS[p][2]
            return own(p, 2, g, ks) + got((p, 1, 1), g * 4 * rows + ks[0] * rows, len(ks) * rows, scales[p])

        for owner in range(1, 16):
            key = ("z", 0, owner)
            put_scale(key, sent)
            put(
                key,
                0,
                jnp.concatenate([summed(p, owner // 4, (owner % 4,)) for p in Z_ALL], axis=0),
                inverse,
            )
            message(key).start()
        for p in Z_ALL:
            keep(p, 2, 0, (0,), summed(p, 0, (0,)))

    def finish(parts, kind, half, count):
        done = len(ORDERS[PARTS[parts[0]][0]])
        block = jnp.concatenate([own(p, done, 0, (0,)) for p in parts], axis=0)
        for tau in range(1, count):
            key = (kind, half, tau)
            message(key).wait_recv()
            block = block + got(key, 0, block.shape[0], scale_in(key))
        row = 0
        for p in parts:
            _, first_row, rows, _ = PARTS[p]
            grad[pl.ds(first_row, rows), lanes_of(p)] = block[row : row + rows]
            row += rows

    second(XY[0])
    second(XY[1])
    second(Z_ALL)
    third(XY[0])
    third(XY[1])
    fourth(0)
    third_z()
    fourth(1)
    finish(XY[0], "xy", 0, 4)
    finish(Z_ALL, "z", 0, 16)
    finish(XY[1], "xy", 1, 4)
    clip[0] = factors[0, 0, 0]
    for key in MESSAGES:
        message(key).wait_send()
    for copy in [mate, *norm_copies]:
        copy.wait_send()


def on_device(mlp_input, mlp_cotangent, head_outputs, out_cotangent):
    threshold = 0.5 * SEQ * math.sqrt(D * FF + 4 * HD * D)
    factor = math.sqrt(D * HD / EXAMPLES) / threshold
    f32, bf16 = jnp.float32, jnp.bfloat16
    dma = pltpu.SemaphoreType.DMA
    return pl.pallas_call(
        functools.partial(kernel, threshold, factor),
        out_shape=(
            jax.ShapeDtypeStruct((OWNED, COLS), f32),
            jax.ShapeDtypeStruct((1,), f32),
        ),
        in_specs=[pl.BlockSpec(memory_space=pl.ANY)] * 4,
        out_specs=(
            pl.BlockSpec(memory_space=pltpu.VMEM),
            pl.BlockSpec(memory_space=pltpu.SMEM),
        ),
        scratch_shapes=[
            pltpu.VMEM((SEQ, D), bf16),
            pltpu.VMEM((SEQ, FF // 4), bf16),
            pltpu.VMEM((SEQ, COLS), bf16),
            pltpu.VMEM((SEQ, D), bf16),
            pltpu.VMEM((D, 256), f32),
            pltpu.VMEM((D, 256), f32),
            pltpu.VMEM((3, HALF, HALF), f32),
            pltpu.VMEM((3, HALF, HALF), f32),
            pltpu.VMEM((8, COLS), f32),
            pltpu.VMEM((8, COLS), f32),
            pltpu.VMEM((len(PARTS), 8, LANES), f32),
            pltpu.VMEM((MESSAGE_ROWS, LANES), bf16),
            pltpu.VMEM((MESSAGE_ROWS, LANES), bf16),
            pltpu.VMEM((2, 8, LANES), f32),
            pltpu.VMEM((8, LANES), f32),
            pltpu.VMEM((7, 2, 8, LANES), f32),
            pltpu.VMEM((7, 8, LANES), f32),
            dma((2,)),
            dma((3,)),
            dma((2,)),
            dma((len(MESSAGES),)),
            dma((len(MESSAGES),)),
            dma((3,)),
            dma((3,)),
            dma((13,)),
            dma((13,)),
        ],
        compiler_params=pltpu.CompilerParams(
            collective_id=0,
            has_side_effects=True,
            vmem_limit_bytes=56 * 2**20,
        ),
    )(mlp_input, mlp_cotangent, head_outputs, out_cotangent)


def solution(mesh):
    return jax.shard_map(
        on_device,
        mesh=mesh,
        in_specs=(
            P("dp", None, None),
            P("dp", None, "tensor"),
            P("dp", None, "tensor"),
            P("dp", None, None),
        ),
        out_specs=(P("dp", "tensor"), P("dp")),
        check_vma=False,
    )
```
